256 devices in a mesh: pos: 16 (over z, x_hi), var: 16 (over x_lo, y, core).
Axes of the slice: x: 4 (x_hi: 2, x_lo: 2; x = x_hi * 2 + x_lo), y: 4, z: 8, core: 2. Of those that a mesh axis runs over, the one named last changes fastest.
Arguments:
- tower_input: bfloat16 [1024, 1536], P('pos', 'var'), may hold values from -11 to 11
- var_bins: int32 [2048], P(('pos', 'var')), may hold values from 0 to 1023, as said below
- alt_codes: int32 [2048], P(('pos', 'var')), may hold values from 0 to 3
- dilations: int32 [2], replicated, may hold values from 1 to 7, as said below
- base_embed: float32 [4, 1536], replicated, may hold values from -6 to 6
- dw_kernel: float32 [2, 3, 1536], replicated, may hold values from -3 to 3
- norm_gain: float32 [2, 1536], replicated, may hold values from 0.25 to 1.75
- pw_weight: bfloat16 [2, 1536, 1536], replicated, may hold values from -0.15625 to 0.15625
Outputs:
- effects: float32 [2048, 1536], P(('pos', 'var'))
The draws below stay inside these ranges and needn't reach their ends.
Inputs may be any that keep to these rules, and one draw needn't show every extreme that they name: `var_bins`: variant bins cluster around a few centres of the locus. One of the two dilations is 7.
All inputs are finite; a program needn't handle non-finite values.
Results may differ from the reference program's by a relative error of at most 0.004.
The reference program's roundings to bfloat16 on the way count: a program that leaves them out, or rounds other values in their place, can miss the bound.
Values may be sent and summed in bfloat16 or wider, within the bound.
A program may use at most 64 MiB of HBM per device.

```python
import jax
import jax.numpy as jnp
from jax import lax

C = 1536
VAR_DEV = 8
DMAX = 7
CONE = 32
BINS = 1024
VARIANTS = 2048


def draw_tower_input(key, part):
    key = jax.random.fold_in(key, 11)
    first = jax.random.fold_in(key, 0)
    channel = jnp.arange(C, dtype=jnp.float32) / C
    scale = 0.5 * jnp.exp(channel * jnp.log(3.0))
    values = jnp.clip(jax.random.normal(first, (BINS, C), jnp.float32), -4.0, 4.0) * scale[None, :]
    return values.astype(jnp.bfloat16)


def draw_var_bins(key, part):
    key = jax.random.fold_in(key, 12)
    kone, ktwo, kthree = jax.random.split(key, 3)
    centres = jax.random.randint(kone, (8,), 0, BINS)
    which = jax.random.randint(ktwo, (VARIANTS,), 0, 8)
    offsets = jax.random.randint(kthree, (VARIANTS,), -48, 48)
    return jnp.clip(centres[which] + offsets, 0, BINS - 1).astype(jnp.int32)


def draw_dilations(key, part):
    key = jax.random.fold_in(key, 13)
    kone, ktwo = jax.random.split(key)
    other = jax.random.randint(kone, (), 1, DMAX + 1)
    order = jax.random.randint(ktwo, (), 0, 2)
    largest = jnp.array(DMAX, jnp.int32)
    return jnp.where(order == 0, jnp.stack([largest, other]), jnp.stack([other, largest])).astype(jnp.int32)


def with_ends(values, rng, low, high):
    place = [jax.random.randint(jax.random.fold_in(rng, axis), (), 0, length) for axis, length in enumerate(values.shape)]
    widest = values.shape.index(max(values.shape))
    beside = place[:widest] + [(place[widest] + 1) % values.shape[widest]] + place[widest + 1:]
    return values.at[tuple(place)].set(low).at[tuple(beside)].set(high)


def scatter_about(rng, extent, width, limit, kind=jnp.bfloat16):
    values = jax.random.normal(rng, extent, jnp.float32) * width
    return jnp.minimum(jnp.maximum(values, -limit), limit).astype(kind)


def setup_inputs(seed: int = 0) -> dict:
    key_of = jax.random.split(jax.random.key(seed), 9)
    return {
        "tower_input": draw_tower_input(jax.random.fold_in(key_of[8], 71), 0),
        "var_bins": draw_var_bins(jax.random.fold_in(key_of[8], 71), 0),
        "alt_codes": with_ends(jax.random.randint(key_of[2], (VARIANTS,), 0, 4), jax.random.fold_in(key_of[2], 1), 0, 3).astype(jnp.int32),
        "dilations": draw_dilations(jax.random.fold_in(key_of[8], 71), 0),
        "base_embed": scatter_about(key_of[4], (4, C), 1.0, 6.0, jnp.float32),
        "dw_kernel": scatter_about(key_of[5], (2, 3, C), 0.6, 3.0, jnp.float32),
        "norm_gain": jnp.clip(1.0 + 0.15 * jax.random.normal(key_of[6], (2, C), jnp.float32), 0.25, 1.75),
        "pw_weight": scatter_about(key_of[7], (2, C, C), C ** -0.5, 0.15625),
    }


def layer_block(window, start, count, dilation, taps, gain, weight):
    values = window.astype(jnp.float32)
    left = lax.dynamic_slice_in_dim(values, start - dilation, count, 1)
    middle = values[:, start:start + count]
    right = lax.dynamic_slice_in_dim(values, start + dilation, count, 1)
    conv = taps[0] * left + taps[1] * middle + taps[2] * right
    meansq = lax.optimization_barrier(jnp.mean(conv * conv, axis=-1, keepdims=True))
    normed = conv * lax.rsqrt(meansq + 1e-06) * gain
    feature = jax.nn.gelu(normed).astype(jnp.bfloat16)
    batch, rows, chans = feature.shape
    proj = jnp.dot(feature.reshape(batch * rows, chans), weight, preferred_element_type=jnp.float32)
    return middle + proj.reshape(batch, rows, weight.shape[1])

def cone_effect(in_window, one_window, bins, codes, dilations, taps_one, taps_two, norm_gain, pw_weight, base_embed, total_bins):
    outer = CONE + DMAX + 1
    half = CONE // 2
    onehot = (codes[:, None] == jnp.arange(4, dtype=jnp.int32)[None, :]).astype(jnp.float32)
    change = jnp.dot(onehot, base_embed, precision=lax.Precision.HIGHEST)
    marker = (jnp.arange(in_window.shape[1], dtype=jnp.int32) == outer).astype(jnp.float32)
    alt_zero = in_window.astype(jnp.float32) + marker[None, :, None] * change[:, None, :]
    alt_one = layer_block(alt_zero, outer - half, CONE, dilations[0], taps_one, norm_gain[0], pw_weight[0])
    cone_rows = bins[:, None] - half + jnp.arange(CONE, dtype=jnp.int32)[None, :]
    inside = ((cone_rows >= 0) & (cone_rows < total_bins)).astype(jnp.float32)[..., None]
    alt_one = (alt_one * inside).astype(jnp.bfloat16)
    alt_field = jnp.concatenate([one_window[:, :CONE - half], alt_one, one_window[:, 2 * CONE - half:]], axis=1)
    alt_two = layer_block(alt_field, CONE - half, CONE, dilations[1], taps_two, norm_gain[1], pw_weight[1])
    base_two = layer_block(one_window, CONE - half, CONE, dilations[1], taps_two, norm_gain[1], pw_weight[1])
    return lax.optimization_barrier(jnp.sum((alt_two - base_two) * inside, axis=1))

def reference(tower_input, var_bins, alt_codes, dilations, base_embed, dw_kernel, norm_gain, pw_weight):
    outer = CONE + DMAX + 1
    total_bins = tower_input.shape[0]
    padded = jnp.pad(tower_input, ((DMAX, DMAX), (0, 0)))
    strand_taps = [(dw_kernel[0], dw_kernel[1]), (dw_kernel[0][::-1], dw_kernel[1][::-1])]
    firsts = []
    for taps_one, taps_two in strand_taps:
        first = layer_block(padded[None], DMAX, total_bins, dilations[0], taps_one, norm_gain[0], pw_weight[0])[0]
        firsts.append(jnp.pad(first.astype(jnp.bfloat16), ((CONE, CONE), (0, 0))))
    in_padded = jnp.pad(tower_input, ((outer, outer), (0, 0)))

    def one_group(group):
        bins, codes = group
        in_window = jax.vmap(lambda start: lax.dynamic_slice_in_dim(in_padded, start, 2 * outer, 0))(bins)
        total = jnp.zeros((bins.shape[0], tower_input.shape[1]), jnp.float32)
        for strand in range(2):
            one_window = jax.vmap(lambda start: lax.dynamic_slice_in_dim(firsts[strand], start, 2 * CONE, 0))(bins)
            strand_codes = codes if strand == 0 else 3 - codes
            taps_one, taps_two = strand_taps[strand]
            total = total + cone_effect(in_window, one_window, bins, strand_codes, dilations, taps_one, taps_two, norm_gain, pw_weight, base_embed, total_bins)
        return total * (0.5 / CONE)
    groups = (var_bins.reshape(-1, VAR_DEV), alt_codes.reshape(-1, VAR_DEV))
    result = lax.map(one_group, groups)
    return result.reshape(var_bins.shape[0], tower_input.shape[1])
```

```python
import functools

import jax
import jax.numpy as jnp
from jax import lax
from jax.experimental import pallas as pl
from jax.experimental.pallas import tpu as pltpu
from jax.sharding import PartitionSpec as P

DMAX = 7
CONE = 32
VARS = 8
MARGIN = 4 * DMAX
SLABS = 26
MESH = pl.DeviceIdType.MESH


def gelu_of_norm(conv, gain):
    scale = lax.rsqrt(jnp.mean(conv * conv, axis=-1, keepdims=True) + 1e-06)
    normed = conv * scale * gain
    inner = normed * (0.7978845608028654 + (0.7978845608028654 * 0.044715) * (normed * normed))
    half = 0.5 * normed
    return half + half * jnp.tanh(inner)


def pick(scalars, shape):
    row = lax.broadcasted_iota(jnp.int32, shape, len(shape) - 2)
    value = jnp.full(shape, scalars[0], jnp.int32)
    for v in range(1, VARS):
        value = jnp.where(row == v, scalars[v], value)
    return value


def kernel(
    npos,
    nvar,
    bins_ref,
    codes_ref,
    dil_ref,
    tower_ref,
    embed_ref,
    taps_ref,
    gain_ref,
    weight_ref,
    out_ref,
    w_one,
    w_two,
    field,
    padded,
    bins_row,
    bins_all,
    bins_smem,
    stage,
    send,
    recv,
    rows_x,
    feature,
    first,
    w_sem,
    pos_send,
    pos_recv,
    bin_send,
    bin_recv,
    var_send,
    var_recv,
    smem_sem,
):
    block, width = tower_ref.shape
    bins = npos * block
    chans = out_ref.shape[1]
    my_pos = lax.axis_index("pos")
    my_var = lax.axis_index("var")

    load_one = pltpu.make_async_copy(weight_ref.at[0], w_one, w_sem.at[0])
    load_two = pltpu.make_async_copy(weight_ref.at[1], w_two, w_sem.at[1])
    load_one.start()
    load_two.start()

    barrier = pltpu.get_barrier_semaphore()

    @pl.loop(1, npos)
    def _(i):
        pl.semaphore_signal(
            barrier, inc=1, device_id=(lax.rem(my_pos + i, npos), my_var), device_id_type=MESH
        )

    @pl.loop(1, nvar)
    def _(i):
        pl.semaphore_signal(
            barrier, inc=1, device_id=(my_pos, lax.rem(my_var + i, nvar)), device_id_type=MESH
        )

    lane = lax.broadcasted_iota(jnp.int32, (1, 128), 1)
    line = jnp.zeros((1, 128), jnp.int32)
    for v in range(VARS):
        line = jnp.where(lane == v, bins_ref[v], line)
    bins_row[...] = line
    bins_all[pl.ds(my_var, 1), :] = line
    stage[...] = jnp.zeros_like(stage)
    padded[:MARGIN, :] = jnp.zeros((MARGIN, width), jnp.float32)
    padded[MARGIN + bins :, :] = jnp.zeros((MARGIN, width), jnp.float32)
    pl.semaphore_wait(barrier, npos + nvar - 2)

    def bin_copy(to, slot):
        return pltpu.make_async_remote_copy(
            src_ref=bins_row,
            dst_ref=bins_all.at[pl.ds(slot, 1)],
            send_sem=bin_send.at[to],
            recv_sem=bin_recv.at[slot],
            device_id=(my_pos, to),
            device_id_type=MESH,
        )

    def pos_copy(to, slot):
        return pltpu.make_async_remote_copy(
            src_ref=tower_ref,
            dst_ref=field.at[pl.ds(pl.multiple_of(slot * block, block), block)],
            send_sem=pos_send.at[to],
            recv_sem=pos_recv.at[slot],
            device_id=(to, my_var),
            device_id_type=MESH,
        )

    def var_copy(to, slot):
        return pltpu.make_async_remote_copy(
            src_ref=send.at[to],
            dst_ref=recv.at[slot],
            send_sem=var_send.at[to],
            recv_sem=var_recv.at[slot],
            device_id=(my_pos, to),
            device_id_type=MESH,
        )

    @pl.loop(1, nvar)
    def _(i):
        bin_copy(lax.rem(my_var + i, nvar), my_var).start()

    @pl.loop(1, npos)
    def _(i):
        pos_copy(lax.rem(my_pos + i, npos), my_pos).start()

    padded[pl.ds(MARGIN + my_pos * block, block), :] = tower_ref[...].astype(jnp.float32)

    @pl.loop(1, nvar)
    def _(i):
        other = lax.rem(my_var + i, nvar)
        bin_copy(other, other).wait_recv()

    smem_copy = pltpu.make_async_copy(bins_all, bins_smem, smem_sem)
    smem_copy.start()

    @pl.loop(1, npos)
    def _(i):
        other = lax.rem(my_pos + i, npos)
        pos_copy(other, other).wait_recv()
        rows = field[pl.ds(pl.multiple_of(other * block, block), block), :]
        padded[pl.ds(MARGIN + other * block, block), :] = rows.astype(jnp.float32)

    smem_copy.wait()
    d_one, d_two = dil_ref[0], dil_ref[1]
    shifts = [MARGIN + a * d_one + b * d_two for b in range(-2, 3) for a in range(-2, 3)]

    def gather(to):
        for v in range(VARS):
            at = bins_smem[to, v]
            for j, shift in enumerate(shifts):
                stage[j, pl.ds(v, 1), :] = padded[pl.ds(at + shift, 1), :]
        return stage[...].reshape(SLABS * VARS, width).astype(jnp.bfloat16)

    @pl.loop(1, nvar)
    def _(i):
        to = lax.rem(my_var + i, nvar)
        send[to] = gather(to)
        var_copy(to, my_var).start()

    recv[my_var] = gather(my_var)

    shape = (VARS, chans)
    codes = pick([codes_ref[v] for v in range(VARS)], (VARS, 1))
    centre = pick([bins_ref[v] for v in range(VARS)], (VARS, 1))
    changes = []
    for strand in range(2):
        change = jnp.zeros(shape, jnp.float32)
        for code in range(4):
            row = embed_ref[pl.ds(code if strand == 0 else 3 - code, 1), :]
            change = jnp.where(codes == code, row, change)
        changes.append(change)

    @pl.loop(1, nvar)
    def _(i):
        other = lax.rem(my_var + i, nvar)
        var_copy(other, other).wait_recv()

    @pl.loop(0, SLABS // 2)
    def _(q):
        at = pl.ds(pl.multiple_of(q * 16, 16), 16)
        pair = jnp.concatenate([recv[j, at, :] for j in range(nvar)], axis=-1).astype(jnp.float32)
        rows_x[2 * q] = pair[:VARS]
        rows_x[2 * q + 1] = pair[VARS:]

    def taps_of(layer, strand):
        order = (0, 1, 2) if strand == 0 else (2, 1, 0)
        return [taps_ref[layer, pl.ds(t, 1), :] for t in order]

    def put(at, pair):
        where = pl.ds(pl.multiple_of(at * 16, 16), 16)
        feature[where, :] = jnp.concatenate(pair, axis=0).astype(jnp.bfloat16)

    @pl.loop(0, 5)
    def _(b):
        gain = gain_ref[0:1, :]
        for a in range(3):
            pair = []
            for strand in range(2):
                taps = taps_of(0, strand)
                conv = (
                    taps[0] * rows_x[b * 5 + a]
                    + taps[1] * rows_x[b * 5 + a + 1]
                    + taps[2] * rows_x[b * 5 + a + 2]
                )
                pair.append(gelu_of_norm(conv, gain))
            put(b * 3 + a, pair)

    gain = gain_ref[0:1, :]
    for a in range(3):
        pair = []
        for strand in range(2):
            taps = taps_of(0, strand)
            xs = [rows_x[10 + a + t] for t in range(3)]
            xs[2 - a] = xs[2 - a] + changes[strand]
            pair.append(gelu_of_norm(taps[0] * xs[0] + taps[1] * xs[1] + taps[2] * xs[2], gain))
        put(15 + a, pair)

    load_one.wait()

    step = 256 if chans % 256 == 0 else 128

    @pl.loop(0, chans // step)
    def _(n):
        cols = pl.ds(pl.multiple_of(n * step, step), step)
        first[:, cols] = jnp.dot(feature[...], w_one[:, cols], preferred_element_type=jnp.float32)

    def inside(a, b):
        at = centre + (a - 1) * d_one + (b - 2) * d_two
        return (at >= 0) & (at < bins)

    def rounded(value, keep):
        return jnp.where(keep, value, 0.0).astype(jnp.bfloat16).astype(jnp.float32)

    @pl.loop(0, 5)
    def _(b):
        for a in range(3):
            keep = inside(a, b)
            for strand in range(2):
                at = pl.ds(pl.multiple_of((b * 3 + a) * 16 + 8 * strand, 8), 8)
                first[at, :] = rounded(rows_x[b * 5 + a + 1] + first[at, :], keep)

    for a in range(3):
        keep = inside(a, 2)
        for strand in range(2):
            at = pl.ds((15 + a) * 16 + 8 * strand, 8)
            middle = rows_x[11 + a]
            if a == 1:
                middle = middle + changes[strand]
            first[at, :] = rounded(middle + first[at, :], keep)

    same = d_one == d_two
    total = jnp.zeros(shape, jnp.float32)
    moved = jnp.zeros(shape, jnp.float32)
    gain = gain_ref[1:2, :]
    for strand in range(2):
        taps = taps_of(1, strand)

        def ref_at(a, b):
            return first[pl.ds((b * 3 + a) * 16 + 8 * strand, 8), :]

        def new_at(a):
            return first[pl.ds((15 + a) * 16 + 8 * strand, 8), :]

        def alt_at(a, b):
            if b == 2:
                return new_at(a)
            if b > 2 and a + b - 2 <= 2:
                return jnp.where(same, new_at(a + b - 2), ref_at(a, b))
            return ref_at(a, b)

        for a in range(3):
            for b in range(1, 4):
                weight = inside(a, b).astype(jnp.float32)
                if (a, b) in ((1, 1), (1, 2), (2, 1), (2, 2)):
                    weight = jnp.where(same, 0.0, weight)
                olds = [ref_at(a, b + t) for t in (-1, 0, 1)]
                news = [alt_at(a, b + t) for t in (-1, 0, 1)]
                old, new = (
                    gelu_of_norm(taps[0] * r[0] + taps[1] * r[1] + taps[2] * r[2], gain)
                    .astype(jnp.bfloat16)
                    .astype(jnp.float32)
                    for r in (olds, news)
                )
                total = total + weight * (new - old)
                if b >= 2:
                    moved = moved + weight * (news[1] - olds[1])

    high = total.astype(jnp.bfloat16)
    low = (total - high.astype(jnp.float32)).astype(jnp.bfloat16)
    feature[pl.ds(0, 16), :] = jnp.concatenate(
        [high.astype(jnp.float32), low.astype(jnp.float32)], axis=0
    ).astype(jnp.bfloat16)
    out_ref[...] = moved
    load_two.wait()

    @pl.loop(0, chans // step)
    def _(n):
        cols = pl.ds(pl.multiple_of(n * step, step), step)
        both = jnp.dot(
            feature[pl.ds(0, 16), :], w_two[:, cols], preferred_element_type=jnp.float32
        )
        out_ref[:, cols] = (out_ref[:, cols] + (both[:8] + both[8:])) * (0.5 / CONE)

    @pl.loop(1, nvar)
    def _(i):
        other = lax.rem(my_var + i, nvar)
        bin_copy(other, my_var).wait_send()
        var_copy(other, my_var).wait_send()

    @pl.loop(1, npos)
    def _(i):
        pos_copy(lax.rem(my_pos + i, npos), my_pos).wait_send()


def solution(mesh):
    npos, nvar = mesh.shape["pos"], mesh.shape["var"]

    def local(tower, var_bins, alt_codes, dilations, base_embed, dw_kernel, norm_gain, pw_weight):
        block, width = tower.shape
        chans = pw_weight.shape[1]
        bins = npos * block
        smem = pl.BlockSpec(memory_space=pltpu.SMEM)
        vmem = pl.BlockSpec(memory_space=pltpu.VMEM)
        dma = pltpu.SemaphoreType.DMA
        return pl.pallas_call(
            functools.partial(kernel, npos, nvar),
            out_shape=jax.ShapeDtypeStruct((VARS, chans), jnp.float32),
            in_specs=[smem] * 3 + [vmem] * 4 + [pl.BlockSpec(memory_space=pl.ANY)],
            out_specs=vmem,
            scratch_shapes=[
                pltpu.VMEM((chans, chans), jnp.bfloat16),
                pltpu.VMEM((chans, chans), jnp.bfloat16),
                pltpu.VMEM((bins, width), jnp.bfloat16),
                pltpu.VMEM((bins + 2 * MARGIN, width), jnp.float32),
                pltpu.VMEM((1, 128), jnp.int32),
                pltpu.VMEM((nvar, 128), jnp.int32),
                pltpu.SMEM((nvar, 128), jnp.int32),
                pltpu.VMEM((SLABS, VARS, width), jnp.float32),
                pltpu.VMEM((nvar, SLABS * VARS, width), jnp.bfloat16),
                pltpu.VMEM((nvar, SLABS * VARS, width), jnp.bfloat16),
                pltpu.VMEM((SLABS, VARS, chans), jnp.float32),
                pltpu.VMEM((18 * 16, chans), jnp.bfloat16),
                pltpu.VMEM((18 * 16, chans), jnp.float32),
                dma((2,)),
                dma((npos,)),
                dma((npos,)),
                dma((nvar,)),
                dma((nvar,)),
                dma((nvar,)),
                dma((nvar,)),
                dma,
            ],
            compiler_params=pltpu.CompilerParams(
                collective_id=0, has_side_effects=True, vmem_limit_bytes=48 * 1024 * 1024
            ),
        )(var_bins, alt_codes, dilations, tower, base_embed, dw_kernel, norm_gain, pw_weight)

    in_specs = (P("pos", "var"), P(("pos", "var")), P(("pos", "var")), P(), P(), P(), P(), P())
    return jax.shard_map(
        local, mesh=mesh, in_specs=in_specs, out_specs=P(("pos", "var"), None), check_vma=False
    )
```

```python
import functools

import jax
import jax.numpy as jnp
from jax import lax
from jax.experimental import pallas as pl
from jax.experimental.pallas import tpu as pltpu
from jax.sharding import PartitionSpec as P

DMAX = 7
CONE = 32
VARS = 8
MARGIN = 32
TILES = 4
CUT = 2
MESH = pl.DeviceIdType.MESH
STEP = 512


def gelu_of_norm(conv, gain):
    scale = lax.rsqrt(jnp.mean(conv * conv, axis=-1, keepdims=True) + 1e-06)
    normed = conv * scale * gain
    inner = normed * (0.7978845608028654 + (0.7978845608028654 * 0.044715) * (normed * normed))
    half = 0.5 * normed
    return half + half * jnp.tanh(inner)


def pick(scalars, shape):
    row = lax.broadcasted_iota(jnp.int32, shape, len(shape) - 2)
    value = jnp.full(shape, scalars[0], jnp.int32)
    for v in range(1, VARS):
        value = jnp.where(row == v, scalars[v], value)
    return value


def fold(rows, width, lane):
    return [
        jnp.where(lane < width, rows[k], pltpu.roll(rows[3], width - 32 * k, 1)) for k in range(3)
    ]


def unfold(three, width, lane):
    moved = [pltpu.roll(three[k], 128 - width + 32 * k, 1) for k in range(3)]
    last = jnp.where(lane < 64, moved[1], moved[2])
    return list(three) + [jnp.where(lane < 32, moved[0], last)]


def kernel(
    npos,
    nvar,
    bins_hbm,
    codes_hbm,
    dil_hbm,
    tower_hbm,
    embed_hbm,
    taps_hbm,
    gain_hbm,
    weight_ref,
    out_ref,
    bins_ref,
    codes_ref,
    dil_ref,
    tower_ref,
    embed_ref,
    taps_ref,
    gain_ref,
    w_one,
    w_two,
    packed,
    field,
    padded,
    bins_row,
    bins_all,
    bins_smem,
    stage,
    send,
    recv,
    rows_x,
    feature,
    first,
    in_sem,
    w_sem,
    pos_send,
    pos_recv,
    bin_send,
    bin_recv,
    var_send,
    var_recv,
    smem_sem,
    ready,
):
    block, width = tower_ref.shape
    bins = npos * block
    chans = out_ref.shape[1]
    my_pos = lax.axis_index("pos")
    my_var = lax.axis_index("var")

    pairs = (
        (tower_hbm, tower_ref),
        (bins_hbm, bins_ref),
        (dil_hbm, dil_ref),
        (codes_hbm, codes_ref),
        (embed_hbm, embed_ref),
        (taps_hbm, taps_ref),
        (gain_hbm, gain_ref),
    )
    loads = [pltpu.make_async_copy(s, d, in_sem.at[i]) for i, (s, d) in enumerate(pairs)]
    for load in loads:
        load.start()
    barrier = pltpu.get_barrier_semaphore()

    @pl.loop(my_pos + 1, npos)
    def _(i):
        pl.semaphore_signal(barrier, inc=1, device_id=(i, my_var), device_id_type=MESH)

    @pl.loop(my_var + 1, nvar)
    def _(i):
        pl.semaphore_signal(barrier, inc=1, device_id=(my_pos, i), device_id_type=MESH)

    load_one = pltpu.make_async_copy(weight_ref.at[0], w_one, w_sem.at[0])
    load_two = pltpu.make_async_copy(weight_ref.at[1], w_two, w_sem.at[1])
    load_one.start()
    load_two.start()

    def bin_copy(to, slot):
        return pltpu.make_async_remote_copy(
            src_ref=bins_row,
            dst_ref=bins_all.at[pl.ds(slot, 1)],
            send_sem=bin_send.at[to],
            recv_sem=bin_recv.at[slot],
            device_id=(my_pos, to),
            device_id_type=MESH,
        )

    def pos_copy(to, slot):
        return pltpu.make_async_remote_copy(
            src_ref=packed,
            dst_ref=field.at[slot],
            send_sem=pos_send.at[to],
            recv_sem=pos_recv.at[slot],
            device_id=(to, my_var),
            device_id_type=MESH,
        )

    def var_copy(part, to, slot):
        at = pl.ds(0, CUT * TILES * VARS) if part == 0 else pl.ds(CUT * TILES * VARS, (5 - CUT) * TILES * VARS)
        return pltpu.make_async_remote_copy(
            src_ref=send.at[to, at],
            dst_ref=recv.at[slot, at],
            send_sem=var_send.at[part, to],
            recv_sem=var_recv.at[part, slot],
            device_id=(my_pos, to),
            device_id_type=MESH,
        )

    wide_lane = lax.broadcasted_iota(jnp.int32, (VARS, 128), 1)
    two_lane = lax.broadcasted_iota(jnp.int32, (16, 128), 1)
    loads[0].wait()
    own = jnp.concatenate(
        [tower_ref[...].astype(jnp.float32), jnp.zeros((block, 128 - width), jnp.float32)], axis=-1
    )
    quarter = block // 4
    folded = fold([own[quarter * k : quarter * (k + 1)] for k in range(4)], width, two_lane)
    packed[...] = jnp.concatenate(folded, axis=0).astype(jnp.bfloat16)
    loads[1].wait()
    lane = lax.broadcasted_iota(jnp.int32, (1, 128), 1)
    line = jnp.zeros((1, 128), jnp.int32)
    for v in range(VARS):
        line = jnp.where(lane == v, bins_ref[v], line)
    bins_row[...] = line
    bins_all[pl.ds(my_var, 1), :] = line

    @pl.when(my_pos + my_var > 0)
    def _():
        pl.semaphore_wait(barrier, my_pos + my_var)

    @pl.loop(0, my_pos)
    def _(i):
        pl.semaphore_signal(ready.at[my_pos], inc=1, device_id=(i, my_var), device_id_type=MESH)

    @pl.loop(0, my_pos)
    def _(i):
        pos_copy(i, my_pos).start()

    @pl.loop(0, my_var)
    def _(i):
        bin_copy(i, my_var).start()

    padded[:MARGIN, :] = jnp.zeros((MARGIN, 128), jnp.float32)
    padded[MARGIN + bins :, :] = jnp.zeros((MARGIN, 128), jnp.float32)
    padded[pl.ds(pl.multiple_of(MARGIN + my_pos * block, 8), block), :] = own

    def keep_block(i):
        three = field[i].astype(jnp.float32)
        four = unfold([three[quarter * k : quarter * (k + 1)] for k in range(3)], width, two_lane)
        for k in range(4):
            at = pl.multiple_of(MARGIN + i * block + quarter * k, 8)
            padded[pl.ds(at, quarter), :] = four[k]

    loads[2].wait()

    @pl.loop(my_var + 1, nvar)
    def _(i):
        bin_copy(i, i).wait_recv()
        bin_copy(i, my_var).start()

    @pl.loop(my_pos + 1, npos)
    def _(i):
        pl.semaphore_wait(ready.at[i], 1)
        pos_copy(i, my_pos).start()

    @pl.loop(0, my_var)
    def _(i):
        bin_copy(i, i).wait_recv()

    smem_copy = pltpu.make_async_copy(bins_all, bins_smem, smem_sem)
    smem_copy.start()

    @pl.loop(0, my_pos)
    def _(i):
        pos_copy(i, i).wait_recv()
        keep_block(i)

    @pl.loop(my_pos + 1, npos)
    def _(i):
        pos_copy(i, i).wait_recv()
        keep_block(i)

    smem_copy.wait()
    d_one, d_two = dil_ref[0], dil_ref[1]

    def gather(part, to):
        tiles = []
        for b in range(CUT) if part == 0 else range(CUT, 5):
            for v in range(VARS):
                at = bins_smem[to, v] + (MARGIN + (b - 2) * d_two)
                for a in range(5):
                    stage[b * 5 + a, pl.ds(v, 1), :] = padded[pl.ds(at + (a - 2) * d_one, 1), :]
            tiles += fold([stage[b * 5 + a] for a in range(4)], width, wide_lane)
            tiles.append(stage[b * 5 + 4])
        return jnp.concatenate(tiles, axis=0).astype(jnp.bfloat16)

    def part_rows(part):
        return slice(0, CUT * TILES * VARS) if part == 0 else slice(CUT * TILES * VARS, 5 * TILES * VARS)

    for part in range(2):

        @pl.loop(1, nvar)
        def _(i):
            to = lax.rem(my_var + i, nvar)
            send[to, part_rows(part), :] = gather(part, to)
            var_copy(part, to, my_var).start()

        recv[my_var, part_rows(part), :] = gather(part, my_var)

    for load in loads[3:]:
        load.wait()
    shape = (VARS, chans)
    codes = pick([codes_ref[v] for v in range(VARS)], (VARS, 1))
    centre = pick([bins_ref[v] for v in range(VARS)], (VARS, 1))
    changes = []
    for strand in range(2):
        change = jnp.zeros(shape, jnp.float32)
        for code in range(4):
            row = embed_ref[pl.ds(code if strand == 0 else 3 - code, 1), :]
            change = jnp.where(codes == code, row, change)
        changes.append(change)

    def taps_of(layer, strand):
        order = (0, 1, 2) if strand == 0 else (2, 1, 0)
        return [taps_ref[t, pl.ds(layer, 1), :] for t in order]

    def put(at, pair):
        where = pl.ds(pl.multiple_of(at * 16, 16), 16)
        feature[where, :] = jnp.concatenate(pair, axis=0).astype(jnp.bfloat16)

    gain_one = gain_ref[0:1, :]
    step = STEP if chans % STEP == 0 else 128

    def arrive(part):
        @pl.loop(1, nvar)
        def _(i):
            other = lax.rem(my_var + i, nvar)
            var_copy(part, other, other).wait_recv()

    def reference_rows(low, high):
        @pl.loop(low, high)
        def _(b):
            slabs = [[] for _ in range(5)]
            at = pl.ds(pl.multiple_of(b * TILES * VARS, 16), TILES * VARS)
            for j in range(nvar):
                tiles = recv[j, at, :].astype(jnp.float32)
                tiles = [tiles[VARS * k : VARS * (k + 1)] for k in range(TILES)]
                for a, slab in enumerate(unfold(tiles[:3], width, wide_lane) + [tiles[3]]):
                    slabs[a].append(slab[:, :width])
            for a in range(5):
                rows_x[b * 5 + a] = jnp.concatenate(slabs[a], axis=-1)

        @pl.loop(low, high)
        def _(b):
            for a in range(3):
                pair = []
                for strand in range(2):
                    taps = taps_of(0, strand)
                    conv = (
                        taps[0] * rows_x[b * 5 + a]
                        + taps[1] * rows_x[b * 5 + a + 1]
                        + taps[2] * rows_x[b * 5 + a + 2]
                    )
                    pair.append(gelu_of_norm(conv, gain_one))
                put(b * 3 + a, pair)

    def project(low, high):
        @pl.loop(0, chans // step)
        def _(n):
            cols = pl.ds(pl.multiple_of(n * step, step), step)
            first[low:high, cols] = jnp.dot(
                feature[low:high, :], w_one[:, cols], preferred_element_type=jnp.float32
            )

    arrive(0)
    reference_rows(0, CUT)
    load_one.wait()
    project(0, CUT * 48)
    arrive(1)
    reference_rows(CUT, 5)
    for a in range(3):
        pair = []
        for strand in range(2):
            taps = taps_of(0, strand)
            xs = [rows_x[10 + a + t] for t in range(3)]
            xs[2 - a] = xs[2 - a] + changes[strand]
            pair.append(gelu_of_norm(taps[0] * xs[0] + taps[1] * xs[1] + taps[2] * xs[2], gain_one))
        put(15 + a, pair)
    project(CUT * 48, 18 * 16)

    def inside(a, b):
        at = centre + (a - 1) * d_one + (b - 2) * d_two
        return (at >= 0) & (at < bins)

    def rounded(value, keep):
        return jnp.where(keep, value, 0.0).astype(jnp.bfloat16).astype(jnp.float32)

    @pl.loop(0, 5)
    def _(b):
        for a in range(3):
            keep = inside(a, b)
            for strand in range(2):
                at = pl.ds(pl.multiple_of((b * 3 + a) * 16 + 8 * strand, 8), 8)
                first[at, :] = rounded(rows_x[b * 5 + a + 1] + first[at, :], keep)

    for a in range(3):
        keep = inside(a, 2)
        for strand in range(2):
            at = pl.ds((15 + a) * 16 + 8 * strand, 8)
            middle = rows_x[11 + a]
            if a == 1:
                middle = middle + changes[strand]
            first[at, :] = rounded(middle + first[at, :], keep)

    same = d_one == d_two
    total = jnp.zeros(shape, jnp.float32)
    moved = jnp.zeros(shape, jnp.float32)
    gain = gain_ref[1:2, :]
    if True:
        for strand in range(2):
            taps = taps_of(1, strand)

            def ref_at(a, b):
                return first[pl.ds((b * 3 + a) * 16 + 8 * strand, 8), :]

            def new_at(a):
                return first[pl.ds((15 + a) * 16 + 8 * strand, 8), :]

            def alt_at(a, b):
                if b == 2:
                    return new_at(a)
                if b > 2 and a + b - 2 <= 2:
                    return jnp.where(same, new_at(a + b - 2), ref_at(a, b))
                return ref_at(a, b)

            for a in range(3):
                for b in range(1, 4):
                    weight = inside(a, b).astype(jnp.float32)
                    if (a, b) in ((1, 1), (1, 2), (2, 1), (2, 2)):
                        weight = jnp.where(same, 0.0, weight)
                    olds = [ref_at(a, b + t) for t in (-1, 0, 1)]
                    news = [alt_at(a, b + t) for t in (-1, 0, 1)]
                    old, new = (
                        gelu_of_norm(taps[0] * r[0] + taps[1] * r[1] + taps[2] * r[2], gain)
                        .astype(jnp.bfloat16)
                        .astype(jnp.float32)
                        for r in (olds, news)
                    )
                    total = total + weight * (new - old)
                    if b >= 2:
                        moved = moved + weight * (news[1] - olds[1])

    high = total.astype(jnp.bfloat16)
    low = (total - high.astype(jnp.float32)).astype(jnp.bfloat16)
    feature[pl.ds(0, 16), :] = jnp.concatenate(
        [high.astype(jnp.float32), low.astype(jnp.float32)], axis=0
    ).astype(jnp.bfloat16)
    out_ref[...] = moved
    load_two.wait()

    if True:
        @pl.loop(0, chans // step)
        def _(n):
            cols = pl.ds(pl.multiple_of(n * step, step), step)
            both = jnp.dot(
                feature[pl.ds(0, 16), :], w_two[:, cols], preferred_element_type=jnp.float32
            )
            out_ref[:, cols] = (out_ref[:, cols] + (both[:8] + both[8:])) * (0.5 / CONE)

    @pl.loop(1, nvar)
    def _(i):
        other = lax.rem(my_var + i, nvar)
        bin_copy(other, my_var).wait_send()
        var_copy(0, other, my_var).wait_send()
        var_copy(1, other, my_var).wait_send()

    @pl.loop(1, npos)
    def _(i):
        pos_copy(lax.rem(my_pos + i, npos), my_pos).wait_send()


def solution(mesh):
    npos, nvar = mesh.shape["pos"], mesh.shape["var"]

    def local(tower, var_bins, alt_codes, dilations, base_embed, dw_kernel, norm_gain, pw_weight):
        block, width = tower.shape
        chans = pw_weight.shape[1]
        bins = npos * block
        taps = jnp.transpose(dw_kernel, (1, 0, 2))
        vmem = pl.BlockSpec(memory_space=pltpu.VMEM)
        dma = pltpu.SemaphoreType.DMA
        return pl.pallas_call(
            functools.partial(kernel, npos, nvar),
            out_shape=jax.ShapeDtypeStruct((VARS, chans), jnp.float32),
            in_specs=[pl.BlockSpec(memory_space=pltpu.HBM)] * 8,
            out_specs=vmem,
            scratch_shapes=[
                pltpu.SMEM((VARS,), jnp.int32),
                pltpu.SMEM((VARS,), jnp.int32),
                pltpu.SMEM((2,), jnp.int32),
                pltpu.VMEM((block, width), jnp.bfloat16),
                pltpu.VMEM(base_embed.shape, jnp.float32),
                pltpu.VMEM((3, 2, chans), jnp.float32),
                pltpu.VMEM((2, chans), jnp.float32),
                pltpu.VMEM((chans, chans), jnp.bfloat16),
                pltpu.VMEM((chans, chans), jnp.bfloat16),
                pltpu.VMEM((block * 3 // 4, 128), jnp.bfloat16),
                pltpu.VMEM((npos, block * 3 // 4, 128), jnp.bfloat16),
                pltpu.VMEM((bins + 2 * MARGIN, 128), jnp.float32),
                pltpu.VMEM((1, 128), jnp.int32),
                pltpu.VMEM((nvar, 128), jnp.int32),
                pltpu.SMEM((nvar, 128), jnp.int32),
                pltpu.VMEM((25, VARS, 128), jnp.float32),
                pltpu.VMEM((nvar, 5 * TILES * VARS, 128), jnp.bfloat16),
                pltpu.VMEM((nvar, 5 * TILES * VARS, 128), jnp.bfloat16),
                pltpu.VMEM((25, VARS, chans), jnp.float32),
                pltpu.VMEM((18 * 16, chans), jnp.bfloat16),
                pltpu.VMEM((18 * 16, chans), jnp.float32),
                dma((7,)),
                dma((2,)),
                dma((npos,)),
                dma((npos,)),
                dma((nvar,)),
                dma((nvar,)),
                dma((2, nvar)),
                dma((2, nvar)),
                dma,
                pltpu.SemaphoreType.REGULAR((npos,)),
            ],
            compiler_params=pltpu.CompilerParams(
                collective_id=0, has_side_effects=True, vmem_limit_bytes=60 * 1024 * 1024
            ),
        )(var_bins, alt_codes, dilations, tower, base_embed, taps, norm_gain, pw_weight)

    in_specs = (P("pos", "var"), P(("pos", "var")), P(("pos", "var")), P(), P(), P(), P(), P())
    return jax.shard_map(
        local, mesh=mesh, in_specs=in_specs, out_specs=P(("pos", "var"), None), check_vma=False
    )
```

```python
import functools

import jax
import jax.numpy as jnp
from jax import lax
from jax.experimental import pallas as pl
from jax.experimental.pallas import tpu as pltpu
from jax.sharding import PartitionSpec as P

DMAX = 7
CONE = 32
VARS = 8
MARGIN = 32
TILES = 4
PARTS = ((0, 3), (3, 5))
MESH = pl.DeviceIdType.MESH
STEP = 1536


CHUNK = 256


def gelu(normed):
    inner = normed * (0.7978845608028654 + (0.7978845608028654 * 0.044715) * (normed * normed))
    half = 0.5 * normed
    return half + half * jnp.tanh(inner)


def pick(scalars, shape):
    row = lax.broadcasted_iota(jnp.int32, shape, len(shape) - 2)
    value = jnp.full(shape, scalars[0], jnp.int32)
    for v in range(1, VARS):
        value = jnp.where(row == v, scalars[v], value)
    return value


def fold(rows, width, lane):
    return [
        jnp.where(lane < width, rows[k], pltpu.roll(rows[3], width - 32 * k, 1)) for k in range(3)
    ]


def unfold(three, width, lane):
    moved = [pltpu.roll(three[k], 128 - width + 32 * k, 1) for k in range(3)]
    last = jnp.where(lane < 64, moved[1], moved[2])
    return list(three) + [jnp.where(lane < 32, moved[0], last)]


def kernel(
    npos,
    nvar,
    bins_hbm,
    codes_hbm,
    dil_hbm,
    tower_hbm,
    embed_hbm,
    taps_hbm,
    gain_hbm,
    weight_ref,
    out_ref,
    bins_ref,
    codes_ref,
    dil_ref,
    tower_ref,
    embed_ref,
    taps_ref,
    gain_ref,
    w_one,
    w_two,
    packed,
    field,
    padded,
    bins_row,
    bins_all,
    bins_smem,
    stage,
    send,
    recv,
    rows_x,
    conv,
    feature,
    first,
    total,
    change,
    in_sem,
    w_sem,
    pos_send,
    pass_send,
    pos_recv,
    bin_send,
    bin_recv,
    var_send,
    var_recv,
    smem_sem,
    ready,
):
    block, width = tower_ref.shape
    bins = npos * block
    chans = out_ref.shape[1]
    my_pos = lax.axis_index("pos")
    my_var = lax.axis_index("var")

    pairs = (
        (tower_hbm, tower_ref),
        (bins_hbm, bins_ref),
        (dil_hbm, dil_ref),
        (codes_hbm, codes_ref),
        (embed_hbm, embed_ref),
        (taps_hbm, taps_ref),
        (gain_hbm, gain_ref),
    )
    loads = [pltpu.make_async_copy(s, d, in_sem.at[i]) for i, (s, d) in enumerate(pairs)]
    for load in loads:
        load.start()
    barrier = pltpu.get_barrier_semaphore()

    length, half = npos // 2, npos // 4
    my_z, my_side = lax.div(my_pos, 2), lax.rem(my_pos, 2)
    partner = my_pos + 1 - 2 * my_side

    def along(z):
        return 2 * z + my_side

    @pl.loop(my_z + 1, length)
    def _(z):
        pl.semaphore_signal(barrier, inc=1, device_id=(along(z), my_var), device_id_type=MESH)

    @pl.when(my_side == 0)
    def _():
        pl.semaphore_signal(barrier, inc=1, device_id=(partner, my_var), device_id_type=MESH)

    @pl.loop(my_var + 1, nvar)
    def _(i):
        pl.semaphore_signal(barrier, inc=1, device_id=(my_pos, i), device_id_type=MESH)

    load_one = pltpu.make_async_copy(weight_ref.at[0], w_one, w_sem.at[0])
    load_two = pltpu.make_async_copy(weight_ref.at[1], w_two, w_sem.at[1])
    load_one.start()
    load_two.start()

    def bin_copy(to, slot):
        return pltpu.make_async_remote_copy(
            src_ref=bins_row,
            dst_ref=bins_all.at[pl.ds(slot, 1)],
            send_sem=bin_send.at[to],
            recv_sem=bin_recv.at[slot],
            device_id=(my_pos, to),
            device_id_type=MESH,
        )

    def pos_copy(to, slot):
        return pltpu.make_async_remote_copy(
            src_ref=packed,
            dst_ref=field.at[slot],
            send_sem=pos_send.at[to],
            recv_sem=pos_recv.at[slot],
            device_id=(to, my_var),
            device_id_type=MESH,
        )

    def pass_on(slot):
        return pltpu.make_async_remote_copy(
            src_ref=field.at[slot],
            dst_ref=field.at[slot],
            send_sem=pass_send.at[slot],
            recv_sem=pos_recv.at[slot],
            device_id=(partner, my_var),
            device_id_type=MESH,
        )

    def var_copy(part, to, slot):
        low, high = PARTS[part]
        at = pl.ds(low * TILES * VARS, (high - low) * TILES * VARS)
        return pltpu.make_async_remote_copy(
            src_ref=send.at[to, at],
            dst_ref=recv.at[slot, at],
            send_sem=var_send.at[part, to],
            recv_sem=var_recv.at[part, slot],
            device_id=(my_pos, to),
            device_id_type=MESH,
        )

    wide_lane = lax.broadcasted_iota(jnp.int32, (VARS, 128), 1)
    two_lane = lax.broadcasted_iota(jnp.int32, (16, 128), 1)
    loads[0].wait()
    own = jnp.concatenate(
        [tower_ref[...].astype(jnp.float32), jnp.zeros((block, 128 - width), jnp.float32)], axis=-1
    )
    quarter = block // 4
    folded = fold([own[quarter * k : quarter * (k + 1)] for k in range(4)], width, two_lane)
    packed[...] = jnp.concatenate(folded, axis=0).astype(jnp.bfloat16)
    loads[1].wait()
    lane = lax.broadcasted_iota(jnp.int32, (1, 128), 1)
    line = jnp.zeros((1, 128), jnp.int32)
    for v in range(VARS):
        line = jnp.where(lane == v, bins_ref[v], line)
    bins_row[...] = line
    bins_all[pl.ds(my_var, 1), :] = line

    heard = my_z + my_side + my_var

    @pl.when(heard > 0)
    def _():
        pl.semaphore_wait(barrier, heard)

    def say(to):
        pl.semaphore_signal(ready.at[my_pos], inc=1, device_id=(to, my_var), device_id_type=MESH)

    @pl.loop(0, my_z)
    def _(z):
        say(along(z))

    @pl.loop(0, my_z)
    def _(z):
        pos_copy(along(z), my_pos).start()

    @pl.when(my_side == 1)
    def _():
        say(partner)
        pos_copy(partner, my_pos).start()

    @pl.loop(0, my_var)
    def _(i):
        bin_copy(i, my_var).start()

    padded[:MARGIN, :] = jnp.zeros((MARGIN, 128), jnp.float32)
    padded[MARGIN + bins :, :] = jnp.zeros((MARGIN, 128), jnp.float32)
    padded[pl.ds(pl.multiple_of(MARGIN + my_pos * block, 8), block), :] = own

    def keep_block(i):
        three = field[i].astype(jnp.float32)
        four = unfold([three[quarter * k : quarter * (k + 1)] for k in range(3)], width, two_lane)
        for k in range(4):
            at = pl.multiple_of(MARGIN + i * block + quarter * k, 8)
            padded[pl.ds(at, quarter), :] = four[k]

    loads[2].wait()

    def answer(low, high):
        @pl.loop(low, high)
        def _(z):
            pl.semaphore_wait(ready.at[along(z)], 1)
            pos_copy(along(z), my_pos).start()

    def take(low, high):
        @pl.loop(low, high)
        def _(z):
            pos_copy(along(z), along(z)).wait_recv()
            pass_on(along(z)).start()
            keep_block(along(z))

    @pl.when(my_z < half)
    def _():
        answer(my_z + 1, half)

    @pl.when(my_z >= half)
    def _():
        answer(my_z + 1, length)

    @pl.when(my_side == 0)
    def _():
        pl.semaphore_wait(ready.at[partner], 1)
        pos_copy(partner, my_pos).start()

    def answer_bins():
        @pl.loop(my_var + 1, nvar)
        def _(i):
            bin_copy(i, i).wait_recv()
            bin_copy(i, my_var).start()

    @pl.when(my_z < half)
    def _():
        take(0, my_z)
        take(my_z + 1, half)
        answer(half, length)
        answer_bins()
        take(half, length)

    @pl.when(my_z >= half)
    def _():
        answer_bins()
        take(0, half)
        take(half, my_z)
        take(my_z + 1, length)

    @pl.loop(0, my_var)
    def _(i):
        bin_copy(i, i).wait_recv()

    smem_copy = pltpu.make_async_copy(bins_all, bins_smem, smem_sem)
    smem_copy.start()

    @pl.loop(0, length)
    def _(z):
        other = 2 * z + 1 - my_side
        pos_copy(other, other).wait_recv()
        keep_block(other)

    smem_copy.wait()
    d_one, d_two = dil_ref[0], dil_ref[1]

    def gather(part, to):
        tiles = []
        for b in range(*PARTS[part]):
            for v in range(VARS):
                at = bins_smem[to, v] + (MARGIN + (b - 2) * d_two)
                for a in range(5):
                    stage[b * 5 + a, pl.ds(v, 1), :] = padded[pl.ds(at + (a - 2) * d_one, 1), :]
            tiles += fold([stage[b * 5 + a] for a in range(4)], width, wide_lane)
            tiles.append(stage[b * 5 + 4])
        return jnp.concatenate(tiles, axis=0).astype(jnp.bfloat16)

    for part, (low, high) in enumerate(PARTS):
        rows = slice(low * TILES * VARS, high * TILES * VARS)

        @pl.loop(1, nvar)
        def _(i):
            to = lax.rem(my_var + i, nvar)
            send[to, rows, :] = gather(part, to)
            var_copy(part, to, my_var).start()

        recv[my_var, rows, :] = gather(part, my_var)

    for load in loads[3:]:
        load.wait()
    shape = (VARS, chans)
    codes = pick([codes_ref[v] for v in range(VARS)], (VARS, 1))
    centre = pick([bins_ref[v] for v in range(VARS)], (VARS, 1))
    for strand in range(2):
        value = jnp.zeros(shape, jnp.float32)
        for code in range(4):
            row = embed_ref[pl.ds(code if strand == 0 else 3 - code, 1), :]
            value = jnp.where(codes == code, row, value)
        change[strand] = value

    chunks = [slice(k, k + CHUNK) for k in range(0, chans, CHUNK)]
    step = STEP if chans % STEP == 0 else 128
    steps = chans // step

    def arrive(part):
        @pl.loop(1, nvar)
        def _(i):
            other = lax.rem(my_var + i, nvar)
            var_copy(part, other, other).wait_recv()

    def assemble(b):
        slabs = [[] for _ in range(5)]
        at = pl.ds(pl.multiple_of(b * TILES * VARS, 16), TILES * VARS)
        for j in range(nvar):
            tiles = recv[j, at, :].astype(jnp.float32)
            tiles = [tiles[VARS * k : VARS * (k + 1)] for k in range(TILES)]
            for a, slab in enumerate(unfold(tiles[:3], width, wide_lane) + [tiles[3]]):
                slabs[a].append(slab[:, :width])
        for a in range(5):
            rows_x[b * 5 + a] = jnp.concatenate(slabs[a], axis=-1)

    def scales(squares):
        return [lax.rsqrt(jnp.sum(s, axis=-1, keepdims=True) / chans + 1e-06) for s in squares]

    def halves(value):
        return sum(value[:, k : k + 128] for k in range(0, value.shape[1], 128))

    def layer_one(at, xs_of):
        squares = [0.0] * 6
        for cols in chunks:
            taps = [taps_ref[t, 0:1, cols] for t in range(3)]
            for k, value in enumerate(xs_of(cols, taps)):
                conv[k, :, cols] = value
                squares[k] = squares[k] + halves(value * value)
        scale = scales(squares)
        for cols in chunks:
            gain = gain_ref[0:1, cols]
            for a in range(3):
                pair = [gelu(conv[2 * a + s, :, cols] * scale[2 * a + s] * gain) for s in range(2)]
                where = pl.ds(pl.multiple_of((at + a) * 16, 16), 16)
                feature[where, cols] = jnp.concatenate(pair, axis=0).astype(jnp.bfloat16)

    def reference_rows(b):
        def xs_of(cols, taps):
            xs = [rows_x[b * 5 + a, :, cols] for a in range(5)]
            low, high = [taps[0] * x for x in xs], [taps[2] * x for x in xs]
            out = []
            for a in range(3):
                middle = taps[1] * xs[a + 1]
                out += [low[a] + middle + high[a + 2], high[a] + middle + low[a + 2]]
            return out

        layer_one(b * 3, xs_of)

    def alternate_rows():
        def xs_of(cols, taps):
            out = []
            for a in range(3):
                for strand in range(2):
                    xs = [rows_x[10 + a + t, :, cols] for t in range(3)]
                    xs[2 - a] = xs[2 - a] + change[strand, :, cols]
                    first, last = (taps[0], taps[2]) if strand == 0 else (taps[2], taps[0])
                    out.append(first * xs[0] + taps[1] * xs[1] + last * xs[2])
            return out

        layer_one(15, xs_of)

    def project(low, high):
        @pl.loop(0, steps)
        def _(n):
            cols = pl.ds(pl.multiple_of(n * step, step), step)
            first[low:high, cols] = jnp.dot(
                feature[low:high, :], w_one[:, cols], preferred_element_type=jnp.float32
            )

    def inside(a, b):
        at = centre + (a - 1) * d_one + (b - 2) * d_two
        return (at >= 0) & (at < bins)

    def finish(block, middle, keep):
        for strand in range(2):
            at = pl.ds(pl.multiple_of(block * 16 + 8 * strand, 8), 8)
            value = jnp.where(keep, middle(strand) + first[at, :], 0.0)
            first[at, :] = value.astype(jnp.bfloat16).astype(jnp.float32)

    same = d_one == d_two

    def layer_two(a, b, with_moved):
        weight = inside(a, b).astype(jnp.float32)
        if b <= 2:
            weight = jnp.where(same & (a >= 1), 0.0, weight)

        def ref_at(b, strand, cols):
            at = pl.multiple_of((b * 3 + a) * 16 + 8 * strand, 8)
            return first[pl.ds(at, 8), cols]

        def new_at(a, strand, cols):
            at = pl.multiple_of((15 + a) * 16 + 8 * strand, 8)
            return first[pl.ds(at, 8), cols]

        def both(strand, cols):
            olds = [ref_at(b + t, strand, cols) for t in (-1, 0, 1)]
            news = list(olds)
            for t in range(3):
                at = b + t - 1
                if at == 2:
                    news[t] = new_at(a, strand, cols)
                elif at > 2:
                    other = new_at(jnp.minimum(a + at - 2, 2), strand, cols)
                    news[t] = jnp.where(same & (a + at - 2 <= 2), other, olds[t])
            return olds, news

        squares = [0.0] * 4
        for cols in chunks:
            taps = [taps_ref[t, 1:2, cols] for t in range(3)]
            for strand in range(2):
                order = taps if strand == 0 else taps[::-1]
                olds, news = both(strand, cols)
                if b >= 2:
                    moved = weight * (news[1] - olds[1])
                    out_ref[:, cols] = out_ref[:, cols] + moved
                old = [k * x for k, x in zip(order, olds)]
                new = [p if x is y else k * y for k, p, x, y in zip(order, old, olds, news)]
                for k, (p, q, r) in enumerate((old, new)):
                    value = p + q + r
                    conv[2 * strand + k, :, cols] = value
                    squares[2 * strand + k] = squares[2 * strand + k] + halves(value * value)
        scale = scales(squares)
        for cols in chunks:
            gain = gain_ref[1:2, cols]
            sums = total[:, cols]
            for strand in range(2):
                old, new = (
                    gelu(conv[2 * strand + k, :, cols] * scale[2 * strand + k] * gain)
                    .astype(jnp.bfloat16)
                    .astype(jnp.float32)
                    for k in range(2)
                )
                sums = sums + weight * (new - old)
            total[:, cols] = sums

    total[...] = jnp.zeros_like(total)
    out_ref[...] = jnp.zeros_like(out_ref)

    arrive(0)

    @pl.loop(0, 3)
    def _(b):
        assemble(b)
        reference_rows(b)

    alternate_rows()
    arrive(1)

    @pl.loop(3, 5)
    def _(b):
        assemble(b)
        reference_rows(b)

    load_one.wait()
    project(0, 18 * 16)

    @pl.loop(0, 5)
    def _(b):
        for a in range(3):
            finish(b * 3 + a, lambda strand: rows_x[b * 5 + a + 1], inside(a, b))

    for a in range(3):
        extra = (lambda strand: change[strand]) if a == 1 else (lambda strand: 0.0)
        finish(15 + a, lambda strand: rows_x[11 + a] + extra(strand), inside(a, 2))

    @pl.loop(0, 3)
    def _(a):
        for b in range(1, 4):
            layer_two(a, b, b > 1)

    high = total[...].astype(jnp.bfloat16)
    low = (total[...] - high.astype(jnp.float32)).astype(jnp.bfloat16)
    feature[pl.ds(0, 16), :] = jnp.concatenate(
        [high.astype(jnp.float32), low.astype(jnp.float32)], axis=0
    ).astype(jnp.bfloat16)
    load_two.wait()

    @pl.loop(0, steps)
    def _(n):
        cols = pl.ds(pl.multiple_of(n * step, step), step)
        both = jnp.dot(
            feature[pl.ds(0, 16), :], w_two[:, cols], preferred_element_type=jnp.float32
        )
        out_ref[:, cols] = (out_ref[:, cols] + (both[:8] + both[8:])) * (0.5 / CONE)

    @pl.loop(1, nvar)
    def _(i):
        other = lax.rem(my_var + i, nvar)
        bin_copy(other, my_var).wait_send()
        for part in range(len(PARTS)):
            var_copy(part, other, my_var).wait_send()

    pos_copy(partner, my_pos).wait_send()

    @pl.loop(1, length)
    def _(i):
        to = along(lax.rem(my_z + i, length))
        pos_copy(to, my_pos).wait_send()
        pass_on(to).wait_send()


def solution(mesh):
    npos, nvar = mesh.shape["pos"], mesh.shape["var"]

    def local(tower, var_bins, alt_codes, dilations, base_embed, dw_kernel, norm_gain, pw_weight):
        block, width = tower.shape
        chans = pw_weight.shape[1]
        bins = npos * block
        taps = jnp.transpose(dw_kernel, (1, 0, 2))
        vmem = pl.BlockSpec(memory_space=pltpu.VMEM)
        dma = pltpu.SemaphoreType.DMA
        return pl.pallas_call(
            functools.partial(kernel, npos, nvar),
            out_shape=jax.ShapeDtypeStruct((VARS, chans), jnp.float32),
            in_specs=[pl.BlockSpec(memory_space=pltpu.HBM)] * 8,
            out_specs=vmem,
            scratch_shapes=[
                pltpu.SMEM((VARS,), jnp.int32),
                pltpu.SMEM((VARS,), jnp.int32),
                pltpu.SMEM((2,), jnp.int32),
                pltpu.VMEM((block, width), jnp.bfloat16),
                pltpu.VMEM(base_embed.shape, jnp.float32),
                pltpu.VMEM((3, 2, chans), jnp.float32),
                pltpu.VMEM((2, chans), jnp.float32),
                pltpu.VMEM((chans, chans), jnp.bfloat16),
                pltpu.VMEM((chans, chans), jnp.bfloat16),
                pltpu.VMEM((block * 3 // 4, 128), jnp.bfloat16),
                pltpu.VMEM((npos, block * 3 // 4, 128), jnp.bfloat16),
                pltpu.VMEM((bins + 2 * MARGIN, 128), jnp.float32),
                pltpu.VMEM((1, 128), jnp.int32),
                pltpu.VMEM((nvar, 128), jnp.int32),
                pltpu.SMEM((nvar, 128), jnp.int32),
                pltpu.VMEM((25, VARS, 128), jnp.float32),
                pltpu.VMEM((nvar, 5 * TILES * VARS, 128), jnp.bfloat16),
                pltpu.VMEM((nvar, 5 * TILES * VARS, 128), jnp.bfloat16),
                pltpu.VMEM((25, VARS, chans), jnp.float32),
                pltpu.VMEM((6, VARS, chans), jnp.float32),
                pltpu.VMEM((18 * 16, chans), jnp.bfloat16),
                pltpu.VMEM((18 * 16, chans), jnp.float32),
                pltpu.VMEM((VARS, chans), jnp.float32),
                pltpu.VMEM((2, VARS, chans), jnp.float32),
                dma((7,)),
                dma((2,)),
                dma((npos,)),
                dma((npos,)),
                dma((npos,)),
                dma((nvar,)),
                dma((nvar,)),
                dma((3, nvar)),
                dma((3, nvar)),
                dma,
                pltpu.SemaphoreType.REGULAR((npos,)),
            ],
            compiler_params=pltpu.CompilerParams(
                collective_id=0, has_side_effects=True, vmem_limit_bytes=60 * 1024 * 1024
            ),
        )(var_bins, alt_codes, dilations, tower, base_embed, taps, norm_gain, pw_weight)

    in_specs = (P("pos", "var"), P(("pos", "var")), P(("pos", "var")), P(), P(), P(), P(), P())
    return jax.shard_map(
        local, mesh=mesh, in_specs=in_specs, out_specs=P(("pos", "var"), None), check_vma=False
    )
```

```python
import functools

import jax
import jax.numpy as jnp
from jax import lax
from jax.experimental import pallas as pl
from jax.experimental.pallas import tpu as pltpu
from jax.sharding import PartitionSpec as P

DMAX = 7
CONE = 32
VARS = 8
MARGIN = 32
TILES = 4
PARTS = ((0, 3), (3, 5))
MESH = pl.DeviceIdType.MESH
STEP = 1536


CHUNK = 256


def gelu(normed):
    inner = normed * (0.7978845608028654 + (0.7978845608028654 * 0.044715) * (normed * normed))
    half = 0.5 * normed
    return half + half * jnp.tanh(inner)


def pick(scalars, shape):
    row = lax.broadcasted_iota(jnp.int32, shape, len(shape) - 2)
    value = jnp.full(shape, scalars[0], jnp.int32)
    for v in range(1, VARS):
        value = jnp.where(row == v, scalars[v], value)
    return value


def fold(rows, width, lane):
    return [
        jnp.where(lane < width, rows[k], pltpu.roll(rows[3], width - 32 * k, 1)) for k in range(3)
    ]


def unfold(three, width, lane):
    moved = [pltpu.roll(three[k], 128 - width + 32 * k, 1) for k in range(3)]
    last = jnp.where(lane < 64, moved[1], moved[2])
    return list(three) + [jnp.where(lane < 32, moved[0], last)]


def kernel(
    npos,
    nvar,
    bins_hbm,
    codes_hbm,
    dil_hbm,
    tower_hbm,
    embed_hbm,
    taps_hbm,
    gain_hbm,
    weight_ref,
    out_ref,
    bins_ref,
    codes_ref,
    dil_ref,
    tower_ref,
    embed_ref,
    taps_ref,
    gain_ref,
    w_one,
    w_two,
    packed,
    field,
    padded,
    bins_row,
    bins_all,
    bins_smem,
    stage,
    send,
    recv,
    rows_x,
    conv,
    feature,
    first,
    total,
    change,
    in_sem,
    w_sem,
    pos_send,
    pass_send,
    pos_recv,
    bin_send,
    bin_recv,
    var_send,
    var_recv,
    smem_sem,
    ready,
):
    block, width = tower_ref.shape
    bins = npos * block
    chans = out_ref.shape[1]
    my_pos = lax.axis_index("pos")
    my_var = lax.axis_index("var")

    pairs = (
        (tower_hbm, tower_ref),
        (bins_hbm, bins_ref),
        (dil_hbm, dil_ref),
        (codes_hbm, codes_ref),
        (embed_hbm, embed_ref),
        (taps_hbm, taps_ref),
        (gain_hbm, gain_ref),
    )
    loads = [pltpu.make_async_copy(s, d, in_sem.at[i]) for i, (s, d) in enumerate(pairs)]
    for load in loads:
        load.start()
    barrier = pltpu.get_barrier_semaphore()

    length, half = npos // 2, npos // 4
    my_z, my_side = lax.div(my_pos, 2), lax.rem(my_pos, 2)
    partner = my_pos + 1 - 2 * my_side

    def along(z):
        return 2 * z + my_side

    @pl.loop(my_z + 1, length)
    def _(z):
        pl.semaphore_signal(barrier, inc=1, device_id=(along(z), my_var), device_id_type=MESH)

    @pl.when(my_side == 0)
    def _():
        pl.semaphore_signal(barrier, inc=1, device_id=(partner, my_var), device_id_type=MESH)

    @pl.loop(my_var + 1, nvar)
    def _(i):
        pl.semaphore_signal(barrier, inc=1, device_id=(my_pos, i), device_id_type=MESH)

    load_one = pltpu.make_async_copy(weight_ref.at[0], w_one, w_sem.at[0])
    load_two = pltpu.make_async_copy(weight_ref.at[1], w_two, w_sem.at[1])
    load_one.start()
    load_two.start()

    def bin_copy(to, slot):
        return pltpu.make_async_remote_copy(
            src_ref=bins_row,
            dst_ref=bins_all.at[pl.ds(slot, 1)],
            send_sem=bin_send.at[to],
            recv_sem=bin_recv.at[slot],
            device_id=(my_pos, to),
            device_id_type=MESH,
        )

    def pos_copy(to, slot):
        return pltpu.make_async_remote_copy(
            src_ref=packed,
            dst_ref=field.at[slot],
            send_sem=pos_send.at[to],
            recv_sem=pos_recv.at[slot],
            device_id=(to, my_var),
            device_id_type=MESH,
        )

    def pass_on(slot):
        return pltpu.make_async_remote_copy(
            src_ref=field.at[slot],
            dst_ref=field.at[slot],
            send_sem=pass_send.at[slot],
            recv_sem=pos_recv.at[slot],
            device_id=(partner, my_var),
            device_id_type=MESH,
        )

    def var_copy(part, to, slot):
        low, high = PARTS[part]
        at = pl.ds(low * TILES * VARS, (high - low) * TILES * VARS)
        return pltpu.make_async_remote_copy(
            src_ref=send.at[to, at],
            dst_ref=recv.at[slot, at],
            send_sem=var_send.at[part, to],
            recv_sem=var_recv.at[part, slot],
            device_id=(my_pos, to),
            device_id_type=MESH,
        )

    wide_lane = lax.broadcasted_iota(jnp.int32, (VARS, 128), 1)
    two_lane = lax.broadcasted_iota(jnp.int32, (16, 128), 1)
    loads[0].wait()
    own = jnp.concatenate(
        [tower_ref[...].astype(jnp.float32), jnp.zeros((block, 128 - width), jnp.float32)], axis=-1
    )
    quarter = block // 4
    folded = fold([own[quarter * k : quarter * (k + 1)] for k in range(4)], width, two_lane)
    packed[...] = jnp.concatenate(folded, axis=0).astype(jnp.bfloat16)
    loads[1].wait()
    lane = lax.broadcasted_iota(jnp.int32, (1, 128), 1)
    line = jnp.zeros((1, 128), jnp.int32)
    for v in range(VARS):
        line = jnp.where(lane == v, bins_ref[v], line)
    bins_row[...] = line
    bins_all[pl.ds(my_var, 1), :] = line

    heard = my_z + my_side + my_var

    @pl.when(heard > 0)
    def _():
        pl.semaphore_wait(barrier, heard)

    def say(to):
        pl.semaphore_signal(ready.at[my_pos], inc=1, device_id=(to, my_var), device_id_type=MESH)

    @pl.loop(0, my_z)
    def _(z):
        say(along(z))

    @pl.loop(0, my_z)
    def _(z):
        pos_copy(along(z), my_pos).start()

    @pl.when(my_side == 1)
    def _():
        say(partner)
        pos_copy(partner, my_pos).start()

    @pl.loop(0, my_var)
    def _(i):
        bin_copy(i, my_var).start()

    padded[:MARGIN, :] = jnp.zeros((MARGIN, 128), jnp.float32)
    padded[MARGIN + bins :, :] = jnp.zeros((MARGIN, 128), jnp.float32)
    padded[pl.ds(pl.multiple_of(MARGIN + my_pos * block, 8), block), :] = own

    def keep_block(i):
        three = field[i].astype(jnp.float32)
        four = unfold([three[quarter * k : quarter * (k + 1)] for k in range(3)], width, two_lane)
        for k in range(4):
            at = pl.multiple_of(MARGIN + i * block + quarter * k, 8)
            padded[pl.ds(at, quarter), :] = four[k]

    loads[2].wait()

    def answer(low, high):
        @pl.loop(low, high)
        def _(z):
            pl.semaphore_wait(ready.at[along(z)], 1)
            pos_copy(along(z), my_pos).start()

    def take(low, high):
        @pl.loop(low, high)
        def _(z):
            pos_copy(along(z), along(z)).wait_recv()
            pass_on(along(z)).start()
            keep_block(along(z))

    @pl.when(my_z < half)
    def _():
        answer(my_z + 1, half)

    @pl.when(my_z >= half)
    def _():
        answer(my_z + 1, length)

    @pl.when(my_side == 0)
    def _():
        pl.semaphore_wait(ready.at[partner], 1)
        pos_copy(partner, my_pos).start()

    def answer_bins():
        @pl.loop(my_var + 1, nvar)
        def _(i):
            bin_copy(i, i).wait_recv()
            bin_copy(i, my_var).start()

    @pl.when(my_z < half)
    def _():
        take(0, my_z)
        take(my_z + 1, half)
        answer(half, length)
        answer_bins()
        take(half, length)

    @pl.when(my_z >= half)
    def _():
        answer_bins()
        take(0, half)
        take(half, my_z)
        take(my_z + 1, length)

    @pl.loop(0, my_var)
    def _(i):
        bin_copy(i, i).wait_recv()

    smem_copy = pltpu.make_async_copy(bins_all, bins_smem, smem_sem)
    smem_copy.start()

    @pl.loop(0, length)
    def _(z):
        other = 2 * z + 1 - my_side
        pos_copy(other, other).wait_recv()
        keep_block(other)

    smem_copy.wait()
    d_one, d_two = dil_ref[0], dil_ref[1]

    def gather(part, to):
        tiles = []
        for b in range(*PARTS[part]):
            for v in range(VARS):
                at = bins_smem[to, v] + (MARGIN + (b - 2) * d_two)
                for a in range(5):
                    stage[b * 5 + a, pl.ds(v, 1), :] = padded[pl.ds(at + (a - 2) * d_one, 1), :]
            tiles += fold([stage[b * 5 + a] for a in range(4)], width, wide_lane)
            tiles.append(stage[b * 5 + 4])
        return jnp.concatenate(tiles, axis=0).astype(jnp.bfloat16)

    for part, (low, high) in enumerate(PARTS):
        rows = slice(low * TILES * VARS, high * TILES * VARS)

        @pl.loop(1, nvar)
        def _(i):
            to = lax.rem(my_var + i, nvar)
            send[to, rows, :] = gather(part, to)
            var_copy(part, to, my_var).start()

        recv[my_var, rows, :] = gather(part, my_var)

    for load in loads[3:]:
        load.wait()
    shape = (VARS, chans)
    codes = pick([codes_ref[v] for v in range(VARS)], (VARS, 1))
    centre = pick([bins_ref[v] for v in range(VARS)], (VARS, 1))
    for strand in range(2):
        value = jnp.zeros(shape, jnp.float32)
        for code in range(4):
            row = embed_ref[pl.ds(code if strand == 0 else 3 - code, 1), :]
            value = jnp.where(codes == code, row, value)
        change[strand] = value

    chunks = [slice(k, k + CHUNK) for k in range(0, chans, CHUNK)]
    step = STEP if chans % STEP == 0 else 128
    steps = chans // step

    def arrive(part):
        @pl.loop(1, nvar)
        def _(i):
            other = lax.rem(my_var + i, nvar)
            var_copy(part, other, other).wait_recv()

    def assemble(b):
        slabs = [[] for _ in range(5)]
        at = pl.ds(pl.multiple_of(b * TILES * VARS, 16), TILES * VARS)
        for j in range(nvar):
            tiles = recv[j, at, :].astype(jnp.float32)
            tiles = [tiles[VARS * k : VARS * (k + 1)] for k in range(TILES)]
            for a, slab in enumerate(unfold(tiles[:3], width, wide_lane) + [tiles[3]]):
                slabs[a].append(slab[:, :width])
        for a in range(5):
            rows_x[b * 5 + a] = jnp.concatenate(slabs[a], axis=-1)

    def scales(squares):
        return [lax.rsqrt(jnp.sum(s, axis=-1, keepdims=True) / chans + 1e-06) for s in squares]

    def halves(value):
        return sum(value[:, k : k + 128] for k in range(0, value.shape[1], 128))

    def layer_one(at, xs_of):
        squares = [0.0] * 6
        for cols in chunks:
            taps = [taps_ref[t, 0:1, cols] for t in range(3)]
            for k, value in enumerate(xs_of(cols, taps)):
                conv[k, :, cols] = value
                squares[k] = squares[k] + halves(value * value)
        scale = scales(squares)
        for cols in chunks:
            gain = gain_ref[0:1, cols]
            for a in range(3):
                pair = [gelu(conv[2 * a + s, :, cols] * scale[2 * a + s] * gain) for s in range(2)]
                where = pl.ds(pl.multiple_of((at + a) * 16, 16), 16)
                feature[where, cols] = jnp.concatenate(pair, axis=0).astype(jnp.bfloat16)

    def reference_rows(b):
        def xs_of(cols, taps):
            xs = [rows_x[b * 5 + a, :, cols] for a in range(5)]
            low, high = [taps[0] * x for x in xs], [taps[2] * x for x in xs]
            out = []
            for a in range(3):
                middle = taps[1] * xs[a + 1]
                out += [low[a] + middle + high[a + 2], high[a] + middle + low[a + 2]]
            return out

        layer_one(b * 3, xs_of)

    def alternate_rows():
        def xs_of(cols, taps):
            out = []
            for a in range(3):
                for strand in range(2):
                    xs = [rows_x[10 + a + t, :, cols] for t in range(3)]
                    xs[2 - a] = xs[2 - a] + change[strand, :, cols]
                    first, last = (taps[0], taps[2]) if strand == 0 else (taps[2], taps[0])
                    out.append(first * xs[0] + taps[1] * xs[1] + last * xs[2])
            return out

        layer_one(15, xs_of)

    def project(low, high):
        @pl.loop(0, steps)
        def _(n):
            cols = pl.ds(pl.multiple_of(n * step, step), step)
            first[low:high, cols] = jnp.dot(
                feature[low:high, :], w_one[:, cols], preferred_element_type=jnp.float32
            )

    def inside(a, b):
        at = centre + (a - 1) * d_one + (b - 2) * d_two
        return (at >= 0) & (at < bins)

    def finish(block, middle, keep):
        for strand in range(2):
            at = pl.ds(pl.multiple_of(block * 16 + 8 * strand, 8), 8)
            value = jnp.where(keep, middle(strand) + first[at, :], 0.0)
            first[at, :] = value.astype(jnp.bfloat16).astype(jnp.float32)

    same = d_one == d_two

    def layer_two(a, b, with_moved):
        weight = inside(a, b).astype(jnp.float32)
        if b <= 2:
            weight = jnp.where(same & (a >= 1), 0.0, weight)

        def ref_at(b, strand, cols):
            at = pl.multiple_of((b * 3 + a) * 16 + 8 * strand, 8)
            return first[pl.ds(at, 8), cols]

        def new_at(a, strand, cols):
            at = pl.multiple_of((15 + a) * 16 + 8 * strand, 8)
            return first[pl.ds(at, 8), cols]

        def both(strand, cols):
            olds = [ref_at(b + t, strand, cols) for t in (-1, 0, 1)]
            news = list(olds)
            for t in range(3):
                at = b + t - 1
                if at == 2:
                    news[t] = new_at(a, strand, cols)
                elif at > 2:
                    other = new_at(jnp.minimum(a + at - 2, 2), strand, cols)
                    news[t] = jnp.where(same & (a + at - 2 <= 2), other, olds[t])
            return olds, news

        squares = [0.0] * 4
        for cols in chunks:
            taps = [taps_ref[t, 1:2, cols] for t in range(3)]
            for strand in range(2):
                order = taps if strand == 0 else taps[::-1]
                olds, news = both(strand, cols)
                if b >= 2:
                    moved = weight * (news[1] - olds[1])
                    out_ref[:, cols] = out_ref[:, cols] + moved
                old = [k * x for k, x in zip(order, olds)]
                new = [p if x is y else k * y for k, p, x, y in zip(order, old, olds, news)]
                for k, (p, q, r) in enumerate((old, new)):
                    value = p + q + r
                    conv[2 * strand + k, :, cols] = value
                    squares[2 * strand + k] = squares[2 * strand + k] + halves(value * value)
        scale = scales(squares)
        for cols in chunks:
            gain = gain_ref[1:2, cols]
            sums = total[:, cols]
            for strand in range(2):
                old, new = (
                    gelu(conv[2 * strand + k, :, cols] * scale[2 * strand + k] * gain)
                    .astype(jnp.bfloat16)
                    .astype(jnp.float32)
                    for k in range(2)
                )
                sums = sums + weight * (new - old)
            total[:, cols] = sums

    total[...] = jnp.zeros_like(total)
    out_ref[...] = jnp.zeros_like(out_ref)

    arrive(0)

    @pl.loop(0, 3)
    def _(b):
        assemble(b)
        reference_rows(b)

    alternate_rows()
    arrive(1)

    @pl.loop(3, 5)
    def _(b):
        assemble(b)
        reference_rows(b)

    load_one.wait()
    project(0, 18 * 16)

    @pl.loop(0, 5)
    def _(b):
        for a in range(3):
            finish(b * 3 + a, lambda strand: rows_x[b * 5 + a + 1], inside(a, b))

    for a in range(3):
        extra = (lambda strand: change[strand]) if a == 1 else (lambda strand: 0.0)
        finish(15 + a, lambda strand: rows_x[11 + a] + extra(strand), inside(a, 2))

    @pl.loop(0, 3)
    def _(a):
        for b in range(1, 4):
            layer_two(a, b, b > 1)

    high = total[...].astype(jnp.bfloat16)
    low = (total[...] - high.astype(jnp.float32)).astype(jnp.bfloat16)
    feature[pl.ds(0, 16), :] = jnp.concatenate(
        [high.astype(jnp.float32), low.astype(jnp.float32)], axis=0
    ).astype(jnp.bfloat16)
    load_two.wait()

    @pl.loop(0, steps)
    def _(n):
        cols = pl.ds(pl.multiple_of(n * step, step), step)
        both = jnp.dot(
            feature[pl.ds(0, 16), :], w_two[:, cols], preferred_element_type=jnp.float32
        )
        out_ref[:, cols] = (out_ref[:, cols] + (both[:8] + both[8:])) * (0.5 / CONE)

    @pl.loop(1, nvar)
    def _(i):
        other = lax.rem(my_var + i, nvar)
        bin_copy(other, my_var).wait_send()
        for part in range(len(PARTS)):
            var_copy(part, other, my_var).wait_send()

    pos_copy(partner, my_pos).wait_send()

    @pl.loop(1, length)
    def _(i):
        to = along(lax.rem(my_z + i, length))
        pos_copy(to, my_pos).wait_send()
        pass_on(to).wait_send()


def solution(mesh):
    npos, nvar = mesh.shape["pos"], mesh.shape["var"]

    def local(tower, var_bins, alt_codes, dilations, base_embed, dw_kernel, norm_gain, pw_weight):
        block, width = tower.shape
        chans = pw_weight.shape[1]
        bins = npos * block
        taps = jnp.transpose(dw_kernel, (1, 0, 2))
        vmem = pl.BlockSpec(memory_space=pltpu.VMEM)
        dma = pltpu.SemaphoreType.DMA
        return pl.pallas_call(
            functools.partial(kernel, npos, nvar),
            out_shape=pltpu.VMEM((VARS, chans), jnp.float32),
            in_specs=[pl.BlockSpec(memory_space=pltpu.HBM)] * 8,
            out_specs=vmem,
            scratch_shapes=[
                pltpu.SMEM((VARS,), jnp.int32),
                pltpu.SMEM((VARS,), jnp.int32),
                pltpu.SMEM((2,), jnp.int32),
                pltpu.VMEM((block, width), jnp.bfloat16),
                pltpu.VMEM(base_embed.shape, jnp.float32),
                pltpu.VMEM((3, 2, chans), jnp.float32),
                pltpu.VMEM((2, chans), jnp.float32),
                pltpu.VMEM((chans, chans), jnp.bfloat16),
                pltpu.VMEM((chans, chans), jnp.bfloat16),
                pltpu.VMEM((block * 3 // 4, 128), jnp.bfloat16),
                pltpu.VMEM((npos, block * 3 // 4, 128), jnp.bfloat16),
                pltpu.VMEM((bins + 2 * MARGIN, 128), jnp.float32),
                pltpu.VMEM((1, 128), jnp.int32),
                pltpu.VMEM((nvar, 128), jnp.int32),
                pltpu.SMEM((nvar, 128), jnp.int32),
                pltpu.VMEM((25, VARS, 128), jnp.float32),
                pltpu.VMEM((nvar, 5 * TILES * VARS, 128), jnp.bfloat16),
                pltpu.VMEM((nvar, 5 * TILES * VARS, 128), jnp.bfloat16),
                pltpu.VMEM((25, VARS, chans), jnp.float32),
                pltpu.VMEM((6, VARS, chans), jnp.float32),
                pltpu.VMEM((18 * 16, chans), jnp.bfloat16),
                pltpu.VMEM((18 * 16, chans), jnp.float32),
                pltpu.VMEM((VARS, chans), jnp.float32),
                pltpu.VMEM((2, VARS, chans), jnp.float32),
                dma((7,)),
                dma((2,)),
                dma((npos,)),
                dma((npos,)),
                dma((npos,)),
                dma((nvar,)),
                dma((nvar,)),
                dma((3, nvar)),
                dma((3, nvar)),
                dma,
                pltpu.SemaphoreType.REGULAR((npos,)),
            ],
            compiler_params=pltpu.CompilerParams(
                collective_id=0, has_side_effects=True, vmem_limit_bytes=60 * 1024 * 1024
            ),
        )(var_bins, alt_codes, dilations, tower, base_embed, taps, norm_gain, pw_weight)

    in_specs = (P("pos", "var"), P(("pos", "var")), P(("pos", "var")), P(), P(), P(), P(), P())
    return jax.shard_map(
        local, mesh=mesh, in_specs=in_specs, out_specs=P(("pos", "var"), None), check_vma=False
    )
```

```python
import functools

import jax
import jax.numpy as jnp
from jax import lax
from jax.experimental import pallas as pl
from jax.experimental.pallas import tpu as pltpu
from jax.sharding import PartitionSpec as P

DMAX = 7
CONE = 32
VARS = 8
MARGIN = 32
TILES = 4
PARTS = ((0, 3), (3, 5))
MESH = pl.DeviceIdType.MESH
STEP = 1536


CHUNK = 256


def gelu(normed):
    inner = normed * (0.7978845608028654 + (0.7978845608028654 * 0.044715) * (normed * normed))
    half = 0.5 * normed
    return half + half * jnp.tanh(inner)


def pick(scalars, shape):
    row = lax.broadcasted_iota(jnp.int32, shape, len(shape) - 2)
    value = jnp.full(shape, scalars[0], jnp.int32)
    for v in range(1, VARS):
        value = jnp.where(row == v, scalars[v], value)
    return value


def fold(rows, width, lane):
    return [
        jnp.where(lane < width, rows[k], pltpu.roll(rows[3], width - 32 * k, 1)) for k in range(3)
    ]


def unfold(three, width, lane):
    moved = [pltpu.roll(three[k], 128 - width + 32 * k, 1) for k in range(3)]
    last = jnp.where(lane < 64, moved[1], moved[2])
    return list(three) + [jnp.where(lane < 32, moved[0], last)]


def kernel(
    npos,
    nvar,
    bins_hbm,
    codes_hbm,
    dil_hbm,
    tower_hbm,
    embed_hbm,
    taps_hbm,
    gain_hbm,
    weight_ref,
    out_ref,
    bins_ref,
    codes_ref,
    dil_ref,
    tower_ref,
    embed_ref,
    taps_ref,
    gain_ref,
    w_one,
    w_two,
    packed,
    field,
    padded,
    bins_row,
    bins_all,
    bins_smem,
    stage,
    send,
    recv,
    rows_x,
    conv,
    feature,
    first,
    total,
    change,
    in_sem,
    w_sem,
    pos_send,
    pass_send,
    pos_recv,
    bin_send,
    bin_recv,
    var_send,
    var_recv,
    smem_sem,
    ready,
):
    block, width = tower_ref.shape
    bins = npos * block
    chans = out_ref.shape[1]
    my_pos = lax.axis_index("pos")
    my_var = lax.axis_index("var")

    pairs = (
        (tower_hbm, tower_ref),
        (bins_hbm, bins_ref),
        (dil_hbm, dil_ref),
        (codes_hbm, codes_ref),
        (embed_hbm, embed_ref),
        (taps_hbm, taps_ref),
        (gain_hbm, gain_ref),
    )
    loads = [pltpu.make_async_copy(s, d, in_sem.at[i]) for i, (s, d) in enumerate(pairs)]
    for load in loads:
        load.start()
    barrier = pltpu.get_barrier_semaphore()

    length, half = npos // 2, npos // 4
    my_z, my_side = lax.div(my_pos, 2), lax.rem(my_pos, 2)
    partner = my_pos + 1 - 2 * my_side

    def along(z):
        return 2 * z + my_side

    @pl.loop(my_z + 1, length)
    def _(z):
        pl.semaphore_signal(barrier, inc=1, device_id=(along(z), my_var), device_id_type=MESH)

    @pl.when(my_side == 0)
    def _():
        pl.semaphore_signal(barrier, inc=1, device_id=(partner, my_var), device_id_type=MESH)

    @pl.loop(my_var + 1, nvar)
    def _(i):
        pl.semaphore_signal(barrier, inc=1, device_id=(my_pos, i), device_id_type=MESH)

    load_one = pltpu.make_async_copy(weight_ref.at[0], w_one, w_sem.at[0])
    load_two = pltpu.make_async_copy(weight_ref.at[1], w_two, w_sem.at[1])
    load_one.start()
    load_two.start()

    def bin_copy(to, slot):
        return pltpu.make_async_remote_copy(
            src_ref=bins_row,
            dst_ref=bins_all.at[pl.ds(slot, 1)],
            send_sem=bin_send.at[to],
            recv_sem=bin_recv.at[slot],
            device_id=(my_pos, to),
            device_id_type=MESH,
        )

    def pos_copy(to, slot):
        return pltpu.make_async_remote_copy(
            src_ref=packed,
            dst_ref=field.at[slot],
            send_sem=pos_send.at[to],
            recv_sem=pos_recv.at[slot],
            device_id=(to, my_var),
            device_id_type=MESH,
        )

    def pass_on(slot):
        return pltpu.make_async_remote_copy(
            src_ref=field.at[slot],
            dst_ref=field.at[slot],
            send_sem=pass_send.at[slot],
            recv_sem=pos_recv.at[slot],
            device_id=(partner, my_var),
            device_id_type=MESH,
        )

    def var_copy(part, to, slot):
        low, high = PARTS[part]
        at = pl.ds(low * TILES * VARS, (high - low) * TILES * VARS)
        return pltpu.make_async_remote_copy(
            src_ref=send.at[to, at],
            dst_ref=recv.at[slot, at],
            send_sem=var_send.at[part, to],
            recv_sem=var_recv.at[part, slot],
            device_id=(my_pos, to),
            device_id_type=MESH,
        )

    wide_lane = lax.broadcasted_iota(jnp.int32, (VARS, 128), 1)
    two_lane = lax.broadcasted_iota(jnp.int32, (16, 128), 1)
    loads[0].wait()
    own = jnp.concatenate(
        [tower_ref[...].astype(jnp.float32), jnp.zeros((block, 128 - width), jnp.float32)], axis=-1
    )
    quarter = block // 4
    folded = fold([own[quarter * k : quarter * (k + 1)] for k in range(4)], width, two_lane)
    packed[...] = jnp.concatenate(folded, axis=0).astype(jnp.bfloat16)
    loads[1].wait()
    lane = lax.broadcasted_iota(jnp.int32, (1, 128), 1)
    line = jnp.zeros((1, 128), jnp.int32)
    for v in range(VARS):
        line = jnp.where(lane == v, bins_ref[v], line)
    bins_row[...] = line
    bins_all[pl.ds(my_var, 1), :] = line

    heard = my_z + my_side + my_var

    @pl.when(heard > 0)
    def _():
        pl.semaphore_wait(barrier, heard)

    def say(to):
        pl.semaphore_signal(ready.at[my_pos], inc=1, device_id=(to, my_var), device_id_type=MESH)

    @pl.loop(0, my_z)
    def _(z):
        say(along(z))

    @pl.loop(0, my_z)
    def _(z):
        pos_copy(along(z), my_pos).start()

    @pl.when(my_side == 1)
    def _():
        say(partner)
        pos_copy(partner, my_pos).start()

    @pl.loop(0, my_var)
    def _(i):
        bin_copy(i, my_var).start()

    padded[:MARGIN, :] = jnp.zeros((MARGIN, 128), jnp.float32)
    padded[MARGIN + bins :, :] = jnp.zeros((MARGIN, 128), jnp.float32)
    padded[pl.ds(pl.multiple_of(MARGIN + my_pos * block, 8), block), :] = own

    def keep_block(i):
        three = field[i].astype(jnp.float32)
        four = unfold([three[quarter * k : quarter * (k + 1)] for k in range(3)], width, two_lane)
        for k in range(4):
            at = pl.multiple_of(MARGIN + i * block + quarter * k, 8)
            padded[pl.ds(at, quarter), :] = four[k]

    loads[2].wait()

    def answer(low, high):
        @pl.loop(low, high)
        def _(z):
            pl.semaphore_wait(ready.at[along(z)], 1)
            pos_copy(along(z), my_pos).start()

    def take(low, high):
        @pl.loop(low, high)
        def _(z):
            pos_copy(along(z), along(z)).wait_recv()
            pass_on(along(z)).start()

        @pl.loop(low, high)
        def _(z):
            keep_block(along(z))

    @pl.when(my_z < half)
    def _():
        answer(my_z + 1, half)

    @pl.when(my_z >= half)
    def _():
        answer(my_z + 1, length)

    @pl.when(my_side == 0)
    def _():
        pl.semaphore_wait(ready.at[partner], 1)
        pos_copy(partner, my_pos).start()

    def answer_bins():
        @pl.loop(my_var + 1, nvar)
        def _(i):
            bin_copy(i, i).wait_recv()
            bin_copy(i, my_var).start()

    @pl.when(my_z < half)
    def _():
        take(0, my_z)
        take(my_z + 1, half)
        answer(half, length)
        answer_bins()
        take(half, length)

    @pl.when(my_z >= half)
    def _():
        answer_bins()
        take(0, half)
        take(half, my_z)
        take(my_z + 1, length)

    @pl.loop(0, my_var)
    def _(i):
        bin_copy(i, i).wait_recv()

    smem_copy = pltpu.make_async_copy(bins_all, bins_smem, smem_sem)
    smem_copy.start()

    @pl.loop(0, length)
    def _(z):
        other = 2 * z + 1 - my_side
        pos_copy(other, other).wait_recv()
        keep_block(other)

    smem_copy.wait()
    d_one, d_two = dil_ref[0], dil_ref[1]

    def gather(part, to):
        tiles = []
        for b in range(*PARTS[part]):
            for v in range(VARS):
                at = bins_smem[to, v] + (MARGIN + (b - 2) * d_two)
                for a in range(5):
                    stage[b * 5 + a, pl.ds(v, 1), :] = padded[pl.ds(at + (a - 2) * d_one, 1), :]
            tiles += fold([stage[b * 5 + a] for a in range(4)], width, wide_lane)
            tiles.append(stage[b * 5 + 4])
        return jnp.concatenate(tiles, axis=0).astype(jnp.bfloat16)

    for part, (low, high) in enumerate(PARTS):
        rows = slice(low * TILES * VARS, high * TILES * VARS)

        @pl.loop(1, nvar)
        def _(i):
            to = lax.rem(my_var + 3 * i, nvar)
            send[to, rows, :] = gather(part, to)
            var_copy(part, to, my_var).start()

        recv[my_var, rows, :] = gather(part, my_var)

    for load in loads[3:]:
        load.wait()
    shape = (VARS, chans)
    codes = pick([codes_ref[v] for v in range(VARS)], (VARS, 1))
    centre = pick([bins_ref[v] for v in range(VARS)], (VARS, 1))
    for strand in range(2):
        value = jnp.zeros(shape, jnp.float32)
        for code in range(4):
            row = embed_ref[pl.ds(code if strand == 0 else 3 - code, 1), :]
            value = jnp.where(codes == code, row, value)
        change[strand] = value

    chunks = [slice(k, k + CHUNK) for k in range(0, chans, CHUNK)]
    step = STEP if chans % STEP == 0 else 128
    steps = chans // step

    def arrive(part):
        @pl.loop(1, nvar)
        def _(i):
            other = lax.rem(my_var + i, nvar)
            var_copy(part, other, other).wait_recv()

    def assemble(b):
        slabs = [[] for _ in range(5)]
        at = pl.ds(pl.multiple_of(b * TILES * VARS, 16), TILES * VARS)
        for j in range(nvar):
            tiles = recv[j, at, :].astype(jnp.float32)
            tiles = [tiles[VARS * k : VARS * (k + 1)] for k in range(TILES)]
            for a, slab in enumerate(unfold(tiles[:3], width, wide_lane) + [tiles[3]]):
                slabs[a].append(slab[:, :width])
        for a in range(5):
            rows_x[b * 5 + a] = jnp.concatenate(slabs[a], axis=-1)

    def scales(squares):
        return [lax.rsqrt(jnp.sum(s, axis=-1, keepdims=True) / chans + 1e-06) for s in squares]

    def halves(value):
        return sum(value[:, k : k + 128] for k in range(0, value.shape[1], 128))

    def layer_one(at, xs_of):
        squares = [0.0] * 6
        for cols in chunks:
            taps = [taps_ref[t, 0:1, cols] for t in range(3)]
            for k, value in enumerate(xs_of(cols, taps)):
                conv[k, :, cols] = value
                squares[k] = squares[k] + halves(value * value)
        scale = scales(squares)
        for cols in chunks:
            gain = gain_ref[0:1, cols]
            for a in range(3):
                pair = [gelu(conv[2 * a + s, :, cols] * scale[2 * a + s] * gain) for s in range(2)]
                where = pl.ds(pl.multiple_of((at + a) * 16, 16), 16)
                feature[where, cols] = jnp.concatenate(pair, axis=0).astype(jnp.bfloat16)

    def reference_rows(b):
        def xs_of(cols, taps):
            xs = [rows_x[b * 5 + a, :, cols] for a in range(5)]
            low, high = [taps[0] * x for x in xs], [taps[2] * x for x in xs]
            out = []
            for a in range(3):
                middle = taps[1] * xs[a + 1]
                out += [low[a] + middle + high[a + 2], high[a] + middle + low[a + 2]]
            return out

        layer_one(b * 3, xs_of)

    def alternate_rows():
        def xs_of(cols, taps):
            out = []
            for a in range(3):
                for strand in range(2):
                    xs = [rows_x[10 + a + t, :, cols] for t in range(3)]
                    xs[2 - a] = xs[2 - a] + change[strand, :, cols]
                    first, last = (taps[0], taps[2]) if strand == 0 else (taps[2], taps[0])
                    out.append(first * xs[0] + taps[1] * xs[1] + last * xs[2])
            return out

        layer_one(15, xs_of)

    def project(low, high):
        @pl.loop(0, steps)
        def _(n):
            cols = pl.ds(pl.multiple_of(n * step, step), step)
            first[low:high, cols] = jnp.dot(
                feature[low:high, :], w_one[:, cols], preferred_element_type=jnp.float32
            )

    def inside(a, b):
        at = centre + (a - 1) * d_one + (b - 2) * d_two
        return (at >= 0) & (at < bins)

    def finish(block, middle, keep):
        for strand in range(2):
            at = pl.ds(pl.multiple_of(block * 16 + 8 * strand, 8), 8)
            value = jnp.where(keep, middle(strand) + first[at, :], 0.0)
            first[at, :] = value.astype(jnp.bfloat16).astype(jnp.float32)

    same = d_one == d_two

    def layer_two(a, b, with_moved):
        weight = inside(a, b).astype(jnp.float32)
        if b <= 2:
            weight = jnp.where(same & (a >= 1), 0.0, weight)

        def ref_at(b, strand, cols):
            at = pl.multiple_of((b * 3 + a) * 16 + 8 * strand, 8)
            return first[pl.ds(at, 8), cols]

        def new_at(a, strand, cols):
            at = pl.multiple_of((15 + a) * 16 + 8 * strand, 8)
            return first[pl.ds(at, 8), cols]

        def both(strand, cols):
            olds = [ref_at(b + t, strand, cols) for t in (-1, 0, 1)]
            news = list(olds)
            for t in range(3):
                at = b + t - 1
                if at == 2:
                    news[t] = new_at(a, strand, cols)
                elif at > 2:
                    other = new_at(jnp.minimum(a + at - 2, 2), strand, cols)
                    news[t] = jnp.where(same & (a + at - 2 <= 2), other, olds[t])
            return olds, news

        squares = [0.0] * 4
        for cols in chunks:
            taps = [taps_ref[t, 1:2, cols] for t in range(3)]
            for strand in range(2):
                order = taps if strand == 0 else taps[::-1]
                olds, news = both(strand, cols)
                if b >= 2:
                    moved = weight * (news[1] - olds[1])
                    out_ref[:, cols] = out_ref[:, cols] + moved
                old = [k * x for k, x in zip(order, olds)]
                new = [p if x is y else k * y for k, p, x, y in zip(order, old, olds, news)]
                for k, (p, q, r) in enumerate((old, new)):
                    value = p + q + r
                    conv[2 * strand + k, :, cols] = value
                    squares[2 * strand + k] = squares[2 * strand + k] + halves(value * value)
        scale = scales(squares)
        for cols in chunks:
            gain = gain_ref[1:2, cols]
            sums = total[:, cols]
            for strand in range(2):
                old, new = (
                    gelu(conv[2 * strand + k, :, cols] * scale[2 * strand + k] * gain)
                    .astype(jnp.bfloat16)
                    .astype(jnp.float32)
                    for k in range(2)
                )
                sums = sums + weight * (new - old)
            total[:, cols] = sums

    total[...] = jnp.zeros_like(total)
    out_ref[...] = jnp.zeros_like(out_ref)

    arrive(0)

    @pl.loop(0, 3)
    def _(b):
        assemble(b)
        reference_rows(b)

    alternate_rows()
    arrive(1)

    @pl.loop(3, 5)
    def _(b):
        assemble(b)
        reference_rows(b)

    load_one.wait()
    project(0, 18 * 16)

    @pl.loop(0, 5)
    def _(b):
        for a in range(3):
            finish(b * 3 + a, lambda strand: rows_x[b * 5 + a + 1], inside(a, b))

    for a in range(3):
        extra = (lambda strand: change[strand]) if a == 1 else (lambda strand: 0.0)
        finish(15 + a, lambda strand: rows_x[11 + a] + extra(strand), inside(a, 2))

    @pl.loop(0, 3)
    def _(a):
        for b in range(1, 4):
            layer_two(a, b, b > 1)

    high = total[...].astype(jnp.bfloat16)
    low = (total[...] - high.astype(jnp.float32)).astype(jnp.bfloat16)
    feature[pl.ds(0, 16), :] = jnp.concatenate(
        [high.astype(jnp.float32), low.astype(jnp.float32)], axis=0
    ).astype(jnp.bfloat16)
    load_two.wait()

    @pl.loop(0, steps)
    def _(n):
        cols = pl.ds(pl.multiple_of(n * step, step), step)
        both = jnp.dot(
            feature[pl.ds(0, 16), :], w_two[:, cols], preferred_element_type=jnp.float32
        )
        out_ref[:, cols] = (out_ref[:, cols] + (both[:8] + both[8:])) * (0.5 / CONE)

    @pl.loop(1, nvar)
    def _(i):
        other = lax.rem(my_var + i, nvar)
        bin_copy(other, my_var).wait_send()
        for part in range(len(PARTS)):
            var_copy(part, other, my_var).wait_send()

    pos_copy(partner, my_pos).wait_send()

    @pl.loop(1, length)
    def _(i):
        to = along(lax.rem(my_z + i, length))
        pos_copy(to, my_pos).wait_send()
        pass_on(to).wait_send()


def solution(mesh):
    npos, nvar = mesh.shape["pos"], mesh.shape["var"]

    def local(tower, var_bins, alt_codes, dilations, base_embed, dw_kernel, norm_gain, pw_weight):
        block, width = tower.shape
        chans = pw_weight.shape[1]
        bins = npos * block
        taps = jnp.transpose(dw_kernel, (1, 0, 2))
        vmem = pl.BlockSpec(memory_space=pltpu.VMEM)
        dma = pltpu.SemaphoreType.DMA
        return pl.pallas_call(
            functools.partial(kernel, npos, nvar),
            out_shape=pltpu.VMEM((VARS, chans), jnp.float32),
            in_specs=[pl.BlockSpec(memory_space=pltpu.HBM)] * 8,
            out_specs=vmem,
            scratch_shapes=[
                pltpu.SMEM((VARS,), jnp.int32),
                pltpu.SMEM((VARS,), jnp.int32),
                pltpu.SMEM((2,), jnp.int32),
                pltpu.VMEM((block, width), jnp.bfloat16),
                pltpu.VMEM(base_embed.shape, jnp.float32),
                pltpu.VMEM((3, 2, chans), jnp.float32),
                pltpu.VMEM((2, chans), jnp.float32),
                pltpu.VMEM((chans, chans), jnp.bfloat16),
                pltpu.VMEM((chans, chans), jnp.bfloat16),
                pltpu.VMEM((block * 3 // 4, 128), jnp.bfloat16),
                pltpu.VMEM((npos, block * 3 // 4, 128), jnp.bfloat16),
                pltpu.VMEM((bins + 2 * MARGIN, 128), jnp.float32),
                pltpu.VMEM((1, 128), jnp.int32),
                pltpu.VMEM((nvar, 128), jnp.int32),
                pltpu.SMEM((nvar, 128), jnp.int32),
                pltpu.VMEM((25, VARS, 128), jnp.float32),
                pltpu.VMEM((nvar, 5 * TILES * VARS, 128), jnp.bfloat16),
                pltpu.VMEM((nvar, 5 * TILES * VARS, 128), jnp.bfloat16),
                pltpu.VMEM((25, VARS, chans), jnp.float32),
                pltpu.VMEM((6, VARS, chans), jnp.float32),
                pltpu.VMEM((18 * 16, chans), jnp.bfloat16),
                pltpu.VMEM((18 * 16, chans), jnp.float32),
                pltpu.VMEM((VARS, chans), jnp.float32),
                pltpu.VMEM((2, VARS, chans), jnp.float32),
                dma((7,)),
                dma((2,)),
                dma((npos,)),
                dma((npos,)),
                dma((npos,)),
                dma((nvar,)),
                dma((nvar,)),
                dma((3, nvar)),
                dma((3, nvar)),
                dma,
                pltpu.SemaphoreType.REGULAR((npos,)),
            ],
            compiler_params=pltpu.CompilerParams(
                collective_id=0, has_side_effects=True, vmem_limit_bytes=60 * 1024 * 1024
            ),
        )(var_bins, alt_codes, dilations, tower, base_embed, taps, norm_gain, pw_weight)

    in_specs = (P("pos", "var"), P(("pos", "var")), P(("pos", "var")), P(), P(), P(), P(), P())
    return jax.shard_map(
        local, mesh=mesh, in_specs=in_specs, out_specs=P(("pos", "var"), None), check_vma=False
    )
```
